256 devices in a mesh: dp: 32 (over y, z_hi, core), mp: 8 (over z_lo, x).
Axes of the slice: x: 4, y: 4, z: 8 (z_hi: 4, z_lo: 2; z = z_hi * 2 + z_lo), core: 2. Of those that a mesh axis runs over, the one named last changes fastest.
Arguments:
- image_map: bfloat16 [32, 16, 16, 3072], P('dp', None, None, 'mp'), may hold values from -6 to 6
- conv_weight: bfloat16 [7, 7, 3072], P(None, None, 'mp'), may hold values from -0.875 to 0.875
- conv_bias: float32 [3072], P('mp'), may hold values from -3 to 3
- ln_gain: float32 [3072], P('mp'), may hold values from 0.25 to 1.75
- ln_bias: float32 [3072], P('mp'), may hold values from -3 to 3
- connector: bfloat16 [3072, 7168], P('mp'), may hold values from -0.109375 to 0.109375
- connector_bias: float32 [7168], replicated, may hold values from -3 to 3
- norm_gain: float32 [7168], replicated, may hold values from 0.25 to 1.75
- q_weight: bfloat16 [7168, 7168], P('dp', 'mp'), may hold values from -1 to 1
- kv_weight: bfloat16 [7168, 8, 2, 128], P(None, 'mp'), may hold values from -1 to 1
- text_hidden: bfloat16 [192, 128, 7168], P('dp', None, 'mp'), may hold values from -6 to 6
- rollout_group: int32 [192], P('dp'), may hold values from 0 to 31
- text_length: int32 [192], P('dp'), may hold values from 1 to 128
Outputs:
- attended: bfloat16 [192, 128, 7168], P('dp', None, 'mp')
- text_cache: bfloat16 [192, 128, 8, 2, 128], P('dp', None, 'mp')
- visual_cache: bfloat16 [32, 64, 8, 2, 128], P('dp', None, 'mp')
The draws below stay inside these ranges and needn't reach their ends.
All inputs are finite; a program needn't handle non-finite values.
Results may differ from the reference program's by a relative error of at most 0.015.
Values may be sent and summed in bfloat16 or wider, within the bound.
A program may use at most 128 MiB of HBM per device.

```python
import jax
import jax.numpy as jnp
from jax import lax

D = 7168
C = 3072
QH = 56
KVH = 8
HD = 128
MAP = 16
KSZ = 7
SEG = 128
VIS = 64
GQ = 7
ROLLOUTS = 192
N_DP = 32


def shared_keys(key):
    spread = jax.random.normal(key, (D, KVH, HD), jnp.float32)
    return jnp.clip(spread, -6.0, 6.0) * D ** (-0.5)


def draw_kv_weight(key, part):
    key_part = shared_keys(key)
    key = jax.random.fold_in(key, 11)
    value_part = jnp.clip(jax.random.normal(key, (D, KVH, HD), jnp.float32), -6.0, 6.0) * D ** (-0.5)
    stacked = jnp.stack([key_part, value_part], axis=2)
    return jnp.clip(stacked, -1.0, 1.0).astype(jnp.bfloat16)


def draw_q_weight(key, part):
    key = jax.random.fold_in(key, 12)
    noise = jnp.clip(jax.random.normal(key, (D, QH, HD), jnp.float32), -6.0, 6.0) * D ** (-0.5)
    return jnp.clip(noise, -1.0, 1.0).reshape(D, QH * HD).astype(jnp.bfloat16)


def draw_text_hidden(key, part):
    key = jax.random.fold_in(key, 13)
    values = jax.random.normal(key, (ROLLOUTS, SEG, D), jnp.float32)
    return jnp.clip(values, -6.0, 6.0).astype(jnp.bfloat16)


def set_ends(entries, stream_key, low, high):
    longest = entries.shape.index(max(entries.shape))
    spots = []
    for shift in (0, 1):
        where = [jax.random.randint(jax.random.fold_in(stream_key, axis), (), 0, length) for axis, length in enumerate(entries.shape)]
        where[longest] = (where[longest] + shift) % entries.shape[longest]
        spots.append(tuple(where))
    return entries.at[spots[0]].set(low).at[spots[1]].set(high)


def shard_levels(rng, shape, shards, low, top_value):
    factor_of, own = 1.0, jax.random.fold_in(rng, 6)
    for dim, blocks in shards:
        draws = jnp.exp(jax.random.uniform(jax.random.fold_in(own, dim), (blocks,), jnp.float32, low / len(shards), top_value / len(shards)))
        factor_of = factor_of * jnp.repeat(draws, shape[dim] // blocks).reshape([-1 if axis == dim else 1 for axis in range(len(shape))])
    return factor_of


def centred(rng, extent, width, limit, cuts=(), held_as=jnp.bfloat16):
    entries = jax.random.normal(rng, extent, jnp.float32) * width
    if len(cuts) > 0:
        entries = shard_levels(rng, extent, cuts, -0.22, 0.18) * entries
    return jnp.clip(entries, min=-limit, max=limit).astype(held_as)


def setup_inputs(seed: int = 0) -> dict:
    arg_keys = jax.random.split(jax.random.key(seed), 14)
    image_map = centred(arg_keys[0], (N_DP, MAP, MAP, C), 1.0, 6.0, ((0, 32), (3, 8)))
    conv_weight = centred(arg_keys[1], (KSZ, KSZ, C), (KSZ * KSZ) ** -0.5, 0.875, ((2, 8),))
    conv_bias = centred(arg_keys[2], (C,), 0.5, 3.0, ((0, 8),), jnp.float32)
    ln_gain = jnp.clip(1.0 + 0.15 * jax.random.normal(arg_keys[3], (C,), jnp.float32), 0.25, 1.75)
    ln_bias = centred(arg_keys[4], (C,), 0.5, 3.0, ((0, 8),), jnp.float32)
    connector = centred(arg_keys[5], (C, D), C ** -0.5, 0.109375, ((0, 8),))
    connector_bias = centred(arg_keys[6], (D,), 0.5, 3.0, (), jnp.float32)
    norm_gain = jnp.clip(1.0 + 0.15 * jax.random.normal(arg_keys[7], (D,), jnp.float32), 0.25, 1.75)
    q_weight = draw_q_weight(jax.random.fold_in(arg_keys[13], 71), 0)
    kv_weight = draw_kv_weight(jax.random.fold_in(arg_keys[13], 71), 0)
    text_hidden = draw_text_hidden(jax.random.fold_in(arg_keys[13], 71), 0)
    rollout_group = set_ends(jax.random.randint(arg_keys[11], (ROLLOUTS,), 0, N_DP), jax.random.fold_in(arg_keys[11], 1), 0, N_DP - 1).astype(jnp.int32)
    text_length = set_ends(jax.random.randint(arg_keys[12], (ROLLOUTS,), 1, SEG + 1), jax.random.fold_in(arg_keys[12], 1), 1, SEG).astype(jnp.int32)
    return dict(image_map=image_map, conv_weight=conv_weight, conv_bias=conv_bias, ln_gain=ln_gain, ln_bias=ln_bias, connector=connector, connector_bias=connector_bias, norm_gain=norm_gain, q_weight=q_weight, kv_weight=kv_weight, text_hidden=text_hidden, rollout_group=rollout_group, text_length=text_length)


def rms_rows(rows, gain):
    widened = rows.astype(jnp.float32)
    inverse = lax.rsqrt(lax.optimization_barrier(jnp.mean(widened * widened, axis=-1, keepdims=True)) + 1e-05)
    return (widened * inverse * gain.astype(jnp.float32)).astype(jnp.bfloat16)

def encode_one(picture, conv_weight, conv_bias, ln_gain, ln_bias):
    widened = picture.astype(jnp.float32)
    margin = KSZ // 2
    padded = jnp.pad(widened, ((margin, margin), (margin, margin), (0, 0)))
    taps = conv_weight.astype(jnp.float32)
    conv_sum = jnp.zeros(widened.shape, jnp.float32) + conv_bias.astype(jnp.float32)
    for row_off in range(KSZ):
        for col_off in range(KSZ):
            conv_sum = conv_sum + padded[row_off:row_off + MAP, col_off:col_off + MAP] * taps[row_off, col_off]
    average = lax.optimization_barrier(jnp.sum(conv_sum, axis=-1, keepdims=True)) / C
    second = lax.optimization_barrier(jnp.sum(conv_sum * conv_sum, axis=-1, keepdims=True)) / C
    variance = second - average * average
    normed = (conv_sum - average) * lax.rsqrt(variance + 1e-06) * ln_gain + ln_bias
    pooled = normed.reshape(MAP // 2, 2, MAP // 2, 2, C).mean(axis=(1, 3))
    return pooled.reshape(VIS, C).astype(jnp.bfloat16)

def attend_one(query_heads, seen, valid_rows, allowed):
    key_rows = seen[:, :, 0].astype(jnp.float32)
    value_rows = seen[:, :, 1].astype(jnp.float32)
    scores = jnp.einsum('skgd,tkd->kgst', query_heads.astype(jnp.float32), key_rows) * HD ** (-0.5)
    scores = jnp.where(allowed, scores, -1e+30)
    peak = lax.optimization_barrier(jnp.max(scores, axis=-1, keepdims=True))
    expo = jnp.exp(scores - peak)
    weights = (expo / lax.optimization_barrier(jnp.sum(expo, axis=-1, keepdims=True))).astype(jnp.bfloat16)
    mixed = jnp.einsum('kgst,tkd->skgd', weights.astype(jnp.float32), value_rows)
    mixed = jnp.where(valid_rows[:, None, None, None], mixed, 0.0)
    return mixed.astype(jnp.bfloat16).reshape(SEG, QH * HD)

def reference(image_map, conv_weight, conv_bias, ln_gain, ln_bias, connector, connector_bias, norm_gain, q_weight, kv_weight, text_hidden, rollout_group, text_length):
    pooled = lax.map(lambda picture: encode_one(picture, conv_weight, conv_bias, ln_gain, ln_bias), image_map)
    visual = (jnp.dot(pooled.reshape(N_DP * VIS, C), connector, preferred_element_type=jnp.float32) + connector_bias).astype(jnp.bfloat16)
    visual_normed = rms_rows(visual, norm_gain)
    kv_flat = kv_weight.reshape(D, KVH * 2 * HD)
    visual_cache = jnp.dot(visual_normed, kv_flat, preferred_element_type=jnp.float32).astype(jnp.bfloat16).reshape(N_DP, VIS, KVH, 2, HD)
    text_normed = rms_rows(text_hidden.reshape(ROLLOUTS * SEG, D), norm_gain)
    positions = jnp.arange(SEG, dtype=jnp.int32)
    valid = positions[None, :] < text_length[:, None]
    text_kv = jnp.dot(text_normed, kv_flat, preferred_element_type=jnp.float32).astype(jnp.bfloat16).reshape(ROLLOUTS, SEG, KVH, 2, HD)
    text_cache = jnp.where(valid[:, :, None, None, None], text_kv, jnp.zeros_like(text_kv))
    queries = jnp.dot(text_normed, q_weight, preferred_element_type=jnp.float32).astype(jnp.bfloat16).reshape(ROLLOUTS, SEG, KVH, GQ, HD)
    key_index = jnp.arange(VIS + SEG, dtype=jnp.int32)
    allowed = (key_index[None, :] < VIS) | (key_index[None, :] - VIS <= positions[:, None])

    def per_rollout(items):
        query_heads, own_cache, group_id, valid_rows = items
        group_cache = lax.dynamic_index_in_dim(visual_cache, group_id, 0, keepdims=False)
        seen = jnp.concatenate([group_cache, own_cache], axis=0)
        return attend_one(query_heads, seen, valid_rows, allowed)
    attended = lax.map(per_rollout, (queries, text_cache, rollout_group, valid))
    return (attended, text_cache, visual_cache)
```

```python
import functools

import jax
import jax.numpy as jnp
from jax import lax
from jax.experimental import pallas as pl
from jax.experimental.pallas import tpu as pltpu
from jax.sharding import PartitionSpec as P

MESH = pl.DeviceIdType.MESH
F32 = jnp.float32
BF16 = jnp.bfloat16

D = 7168
C = 3072
HD = 128
KSZ = 7
GQ = 7
SIDE = 16
VIS = 64
KB = 896
ROWS = 768
HALF = 384
QUART = 192
WR = 224
KVW = 256
CL = 384

A_L, A_R, A_Z, B_L, B_R, C_L, C_R, D_L, D_R, D_Z = range(10)


def gather_kernel(
    img, cw, cb, lg, lb, cbias, conn_hbm, w_hbm, kv_hbm, x_hbm,
    q_out, tkv_out, own_out, vis_out,
    xbuf, wbuf, kvbuf, connbuf, pad, conv, stats, ssb, part, rsb, agb, qacc, kvacc,
    loc, x_s, x_r, w1_s, w1_r, w2_s, w2_r, wc_s, wc_r, st_s, st_r, ss_s, ss_r,
    rs_s, rs_r, ag_s, ag_r, v_s, v_r,
):
    dp = lax.axis_index("dp")
    mp = lax.axis_index("mp")
    y, zh, c = dp // 8, (dp // 2) % 4, dp % 2
    zl, x = mp // 4, mp % 4
    other = 1 - zl

    def mp_id(xx, zz):
        return zz * 4 + (xx + 4) % 4

    def dp_id(yy, zz, cc):
        return ((yy + 4) % 4) * 8 + ((zz + 4) % 4) * 2 + cc

    right, left, cross = (dp, mp_id(x + 1, zl)), (dp, mp_id(x - 1, zl)), (dp, mp_id(x, other))
    z_peer = [(dp_id(y, zh + d, c), mp) for d in (1, 2, 3)]
    y_peer = [(dp_id(y + d, zh, c), mp) for d in (1, 2, 3)]
    sib = (dp_id(y, zh, 1 - c), mp)
    mp_peer = [(dp, (mp + d) % 8) for d in range(1, 8)]

    def rcopy(src, dst, s, r, dev):
        return pltpu.make_async_remote_copy(src, dst, s, r, device_id=dev, device_id_type=MESH)

    lc_x = pltpu.make_async_copy(x_hbm, xbuf.at[mp], loc.at[0])
    lc_w = pltpu.make_async_copy(w_hbm, wbuf.at[dp], loc.at[1])
    lc_kv = pltpu.make_async_copy(kv_hbm, kvbuf, loc.at[2])
    lc_cn = pltpu.make_async_copy(conn_hbm, connbuf, loc.at[3])
    for cp in (lc_x, lc_w, lc_cn, lc_kv):
        cp.start()

    bar = pltpu.get_barrier_semaphore()
    peers = mp_peer + z_peer + y_peer + [sib]
    for dev in peers:
        pl.semaphore_signal(bar, inc=1, device_id=dev, device_id_type=MESH)
    pl.semaphore_wait(bar, len(peers))

    def xsend(h, slot, k, r0, rn, dev, src=None):
        piece = xbuf.at[k, h, pl.ds(r0, rn)]
        return rcopy(piece if src is None else src, piece, x_s.at[h, slot], x_r.at[h, slot], dev)

    def send_a(h):
        src = x_hbm.at[h]
        out = [
            xsend(h, A_Z, mp, 0, HALF, cross, src),
            xsend(h, A_L, mp, 0, HALF, right, src),
            xsend(h, A_R, mp, 0, HALF, left, src),
        ]
        for cp in out:
            cp.start()
        return out

    def xrecv(h, slot, k, r0, rn):
        xsend(h, slot, k, r0, rn, left).wait_recv()

    kl, kr, k2 = mp_id(x - 1, zl), mp_id(x + 1, zl), mp_id(x + 2, zl)
    kz, klz, krz, k2z = mp_id(x, other), mp_id(x - 1, other), mp_id(x + 1, other), mp_id(x + 2, other)

    sends = []

    def go(cp):
        cp.start()
        sends.append(cp)

    def wslot(i):
        return wbuf.at[i]

    def wsend(src, i, s, r, dev):
        go(rcopy(src, wslot(i), s, r, dev))

    sends += send_a(0)
    for d in range(3):
        wsend(w_hbm, dp, w1_s.at[d], w1_r.at[d], z_peer[d])
    for d in range(3):
        wsend(w_hbm, dp, w2_s.at[0, d], w2_r.at[0, d], y_peer[d])
    wsend(w_hbm, dp, wc_s.at[0, 0], wc_r.at[0, 0], sib)
    sends += send_a(1)

    pad[...] = jnp.zeros_like(pad)
    pad[3:19, 8:24, :] = img[...].astype(F32)

    def conv_lanes(l, carry):
        lanes = pl.ds(pl.multiple_of(l * 128, 128), 128)
        acc = jnp.zeros((SIDE, SIDE, 128), F32) + cb[:, lanes].reshape(1, 1, 128)
        taps = cw[:, :, lanes].astype(F32)
        for j in range(KSZ):
            cols = pad[:, 5 + j : 21 + j, lanes]
            for i in range(KSZ):
                acc = acc + cols[i : i + SIDE] * taps[i, j : j + 1].reshape(1, 1, 128)
        conv[:, lanes] = acc.reshape(SIDE * SIDE, 128)
        return carry

    lax.fori_loop(0, CL // 128, conv_lanes, 0)
    hi = lax.Precision.HIGHEST
    nt = (((1,), (1,)), ((), ()))
    ones = jnp.ones((8, CL), F32)
    cv = conv[...]
    s1 = lax.dot_general(ones, cv, nt, precision=hi, preferred_element_type=F32)
    s2 = lax.dot_general(ones, cv * cv, nt, precision=hi, preferred_element_type=F32)
    stats[mp, 0:8] = s1
    stats[mp, 8:16] = s2
    for d in range(7):
        go(rcopy(stats.at[mp], stats.at[mp], st_s.at[d], st_r.at[d], mp_peer[d]))

    lc_x.wait()
    ones_b = jnp.ones((8, KB), BF16)
    for h in range(2):
        xv = xbuf[mp, h].astype(F32)
        sq = xv * xv
        sq_hi = sq.astype(BF16)
        sq_lo = (sq - sq_hi.astype(F32)).astype(BF16)
        ssb[mp, :, h * HALF : (h + 1) * HALF] = lax.dot_general(
            ones_b, sq_hi, nt, preferred_element_type=F32
        ) + lax.dot_general(ones_b, sq_lo, nt, preferred_element_type=F32)
    for d in range(7):
        go(rcopy(ssb.at[mp], ssb.at[mp], ss_s.at[d], ss_r.at[d], mp_peer[d]))

    def src_of(d):
        return (mp + 7 - d) % 8

    for d in range(7):
        sd = src_of(d)
        rcopy(stats.at[sd], stats.at[sd], st_s.at[d], st_r.at[d], mp_peer[d]).wait_recv()
    tot = stats[0]
    for k in range(1, 8):
        tot = tot + stats[k]
    avg = tot[0:1] * (1.0 / C)
    var = tot[8:9] * (1.0 / C) - avg * avg
    rstd = lax.rsqrt(var + 1e-06)
    vrow = lax.broadcasted_iota(jnp.int32, (VIS, SIDE * SIDE), 0)
    pix = lax.broadcasted_iota(jnp.int32, (VIS, SIDE * SIDE), 1)
    hit = (vrow // 8 == pix // 32) & (vrow % 8 == (pix % 16) // 2)
    pool = jnp.where(hit, 0.25 * rstd, 0.0)
    shift = jnp.sum(pool * avg, axis=1, keepdims=True)
    mixed = jnp.dot(pool, conv[...], precision=hi, preferred_element_type=F32)
    pooled = ((mixed - shift) * lg[...] + lb[...]).astype(BF16)
    lc_cn.wait()

    def project(j):
        cols = pl.ds(pl.multiple_of(j * KB, 128), KB)
        return jnp.dot(pooled, connbuf[:, cols], preferred_element_type=F32)

    for d in range(7):
        j = (mp + d + 1) % 8
        part[j] = project(j).astype(BF16)
        go(rcopy(part.at[j], rsb.at[mp], rs_s.at[d], rs_r.at[d], mp_peer[d]))
    own_part = project(mp)

    xrecv(0, A_L, kl, 0, HALF)
    go(xsend(0, B_L, kl, 0, QUART, right))
    xrecv(0, A_R, kr, 0, HALF)
    go(xsend(0, B_R, kr, QUART, QUART, left))
    xrecv(0, A_Z, kz, 0, HALF)
    go(xsend(0, C_L, kz, 0, HALF, right))
    go(xsend(0, C_R, kz, 0, HALF, left))

    def from_z(d):
        return dp_id(y, zh - d - 1, c)

    def from_y(e, d):
        return dp_id(y - d - 1, zh - e, c)

    for e in range(1, 4):
        i = from_z(e - 1)
        rcopy(wslot(i), wslot(i), w1_s.at[e - 1], w1_r.at[e - 1], sib).wait_recv()
        for d in range(3):
            wsend(wslot(i), i, w2_s.at[e, d], w2_r.at[e, d], y_peer[d])
        wsend(wslot(i), i, wc_s.at[e, 0], wc_r.at[e, 0], sib)

    summed = own_part + cbias[:, pl.ds(pl.multiple_of(mp * KB, 128), KB)]
    for d in range(7):
        sd = src_of(d)
        rcopy(rsb.at[sd], rsb.at[sd], rs_s.at[d], rs_r.at[d], sib).wait_recv()
        summed = summed + rsb[sd].astype(F32)
    agb[mp] = summed.astype(BF16)
    for d in range(7):
        go(rcopy(agb.at[mp], agb.at[mp], ag_s.at[d], ag_r.at[d], mp_peer[d]))

    xrecv(1, A_L, kl, 0, HALF)
    go(xsend(1, B_L, kl, 0, QUART, right))
    xrecv(1, A_R, kr, 0, HALF)
    go(xsend(1, B_R, kr, QUART, QUART, left))
    xrecv(1, A_Z, kz, 0, HALF)
    go(xsend(1, C_L, kz, 0, HALF, right))
    go(xsend(1, C_R, kz, 0, HALF, left))

    lc_kv.wait()
    for d in range(7):
        sd = src_of(d)
        rcopy(agb.at[sd], agb.at[sd], ag_s.at[d], ag_r.at[d], sib).wait_recv()

    def vis_step(k, carry):
        acc, sq = carry
        v = agb[k]
        vf = v.astype(F32)
        sq = sq + jnp.sum(vf * vf, axis=1, keepdims=True)
        acc = acc + jnp.dot(v, kvbuf[pl.ds(k * KB, KB)], preferred_element_type=F32)
        return acc, sq

    vacc, vsq = lax.fori_loop(0, 8, vis_step, (jnp.zeros((VIS, KVW), F32), jnp.zeros((VIS, 1), F32)))
    vkv = (vacc * lax.rsqrt(vsq * (1.0 / D) + 1e-05)).astype(BF16)
    own_out[...] = vkv
    vis_out[c, y, zh] = vkv
    for d in range(3):
        piece = vis_out.at[c, y, zh]
        go(rcopy(piece, piece, v_s.at[d], v_r.at[d], z_peer[d]))

    xrecv(0, C_L, klz, 0, HALF)
    go(xsend(0, D_L, klz, 0, QUART, right))
    xrecv(0, C_R, krz, 0, HALF)
    go(xsend(0, D_R, krz, QUART, QUART, left))
    xrecv(1, B_L, k2, 0, QUART)
    xrecv(1, B_R, k2, QUART, QUART)
    go(xsend(1, D_Z, k2, 0, HALF, cross))

    for d in range(3):
        piece = vis_out.at[c, y, (zh + 3 - d) % 4]
        rcopy(piece, piece, v_s.at[d], v_r.at[d], sib).wait_recv()
    for d in range(3):
        piece = vis_out.at[c, y]
        go(rcopy(piece, piece, v_s.at[3 + d], v_r.at[3 + d], y_peer[d]))

    for e in range(4):
        for d in range(3):
            i = from_y(e, d)
            rcopy(wslot(i), wslot(i), w2_s.at[e, d], w2_r.at[e, d], sib).wait_recv()
            wsend(wslot(i), i, wc_s.at[e, d + 1], wc_r.at[e, d + 1], sib)

    for d in range(3):
        piece = vis_out.at[c, (y + 3 - d) % 4]
        rcopy(piece, piece, v_s.at[3 + d], v_r.at[3 + d], sib).wait_recv()
    go(rcopy(vis_out.at[c], vis_out.at[c], v_s.at[6], v_r.at[6], sib))

    def kv_part(h, k):
        return jnp.dot(xbuf[k, h], kvbuf[pl.ds(k * KB, KB)], preferred_element_type=F32)

    def q_part(h, k):
        w = wbuf[pl.ds(k * 4, 4)].reshape(KB, KB)
        return jnp.dot(xbuf[k, h], w, preferred_element_type=F32)

    xrecv(0, B_L, k2, 0, QUART)
    xrecv(0, B_R, k2, QUART, QUART)
    for e in range(4):
        for d in range(4):
            i = dp_id(y - d, zh - e, 1 - c)
            rcopy(wslot(i), wslot(i), wc_s.at[e, d], wc_r.at[e, d], sib).wait_recv()
    lc_w.wait()

    qacc[...] = jnp.zeros_like(qacc)
    kvacc[...] = jnp.zeros_like(kvacc)

    def unit(h, k):
        kvacc[h] += kv_part(h, k)
        qacc[h] += q_part(h, k)

    def unit_zl(n, carry):
        h, xx = n // 4, n % 4
        unit(h, zl * 4 + xx)
        return carry

    def unit_zo(n, carry):
        h, xx = n // 4, n % 4
        unit(h, other * 4 + xx)
        return carry

    lax.fori_loop(0, 8, unit_zl, 0)
    xrecv(0, D_L, k2z, 0, QUART)
    xrecv(0, D_R, k2z, QUART, QUART)
    lax.fori_loop(0, 4, unit_zo, 0)
    xrecv(1, C_L, klz, 0, HALF)
    xrecv(1, C_R, krz, 0, HALF)
    xrecv(1, D_Z, k2z, 0, HALF)
    lax.fori_loop(4, 8, unit_zo, 0)

    for d in range(7):
        sd = src_of(d)
        rcopy(ssb.at[sd], ssb.at[sd], ss_s.at[d], ss_r.at[d], sib).wait_recv()
    ss = ssb[0]
    for k in range(1, 8):
        ss = ss + ssb[k]
    inv = lax.rsqrt(ss * (1.0 / D) + 1e-05)
    inv = jnp.transpose(jnp.broadcast_to(inv[0:1], (128, ROWS)))
    for h in range(2):
        scale = inv[h * HALF : (h + 1) * HALF, 0:1]
        q_out[h] = (qacc[h] * scale).astype(BF16)
        tkv_out[h] = (kvacc[h] * scale).astype(BF16)

    rcopy(vis_out.at[1 - c], vis_out.at[1 - c], v_s.at[6], v_r.at[6], sib).wait_recv()
    for cp in sends:
        cp.wait_send()


def gather_call(img, cw, cb, lg, lb, cbias, conn, w, kv, text):
    vm = pl.BlockSpec(memory_space=pltpu.VMEM)
    hb = pl.BlockSpec(memory_space=pl.ANY)
    dma = pltpu.SemaphoreType.DMA
    return pl.pallas_call(
        gather_kernel,
        out_shape=(
            jax.ShapeDtypeStruct((2, HALF, KB), BF16),
            jax.ShapeDtypeStruct((2, HALF, KVW), BF16),
            jax.ShapeDtypeStruct((VIS, KVW), BF16),
            jax.ShapeDtypeStruct((2, 4, 4, VIS, KVW), BF16),
        ),
        in_specs=[vm] * 6 + [hb] * 4,
        out_specs=(vm,) * 4,
        scratch_shapes=[
            pltpu.VMEM((8, 2, HALF, KB), BF16),
            pltpu.VMEM((32, WR, KB), BF16),
            pltpu.VMEM((D, KVW), BF16),
            pltpu.VMEM((CL, D), BF16),
            pltpu.VMEM((22, 32, CL), F32),
            pltpu.VMEM((SIDE * SIDE, CL), F32),
            pltpu.VMEM((8, 16, SIDE * SIDE), F32),
            pltpu.VMEM((8, 8, ROWS), F32),
            pltpu.VMEM((8, VIS, KB), BF16),
            pltpu.VMEM((8, VIS, KB), BF16),
            pltpu.VMEM((8, VIS, KB), BF16),
            pltpu.VMEM((2, HALF, KB), F32),
            pltpu.VMEM((2, HALF, KVW), F32),
            dma((4,)),
            dma((2, 10)), dma((2, 10)),
            dma((3,)), dma((3,)),
            dma((4, 3)), dma((4, 3)),
            dma((4, 4)), dma((4, 4)),
            dma((7,)), dma((7,)),
            dma((7,)), dma((7,)),
            dma((7,)), dma((7,)),
            dma((7,)), dma((7,)),
            dma((7,)), dma((7,)),
        ],
        compiler_params=pltpu.CompilerParams(
            collective_id=0, has_side_effects=True, vmem_limit_bytes=56 * 2**20
        ),
        cost_estimate=pl.CostEstimate(
            flops=14 * 10**9, bytes_accessed=30 * 10**6, transcendentals=0
        ),
        name="gather",
    )(img, cw, cb, lg, lb, cbias, conn, w, kv, text)


def attend_kernel(slot, length, q_ref, t_ref, v_ref, out_ref, cache_ref):
    n = length[pl.program_id(0)]
    seg = q_ref.shape[1]
    rows = lax.broadcasted_iota(jnp.int32, (seg, 1), 0)
    live = rows < n
    text = jnp.where(live, t_ref[0].astype(F32), 0.0).astype(BF16)
    cache_ref[0] = text
    vis = v_ref[0]
    keys = jnp.concatenate([vis[:, :HD], text[:, :HD]], axis=0)
    vals = jnp.concatenate([vis[:, HD:], text[:, HD:]], axis=0)
    qi = lax.broadcasted_iota(jnp.int32, (seg, VIS + seg), 0)
    ki = lax.broadcasted_iota(jnp.int32, (seg, VIS + seg), 1)
    allowed = ki - VIS <= qi
    nt = (((1,), (1,)), ((), ()))
    for g in range(GQ):
        q = q_ref[0, :, g * HD : (g + 1) * HD]
        s = lax.dot_general(q, keys, nt, preferred_element_type=F32) * HD ** (-0.5)
        s = jnp.where(allowed, s, -1e30)
        e = jnp.exp(s - jnp.max(s, axis=-1, keepdims=True))
        w = (e / jnp.sum(e, axis=-1, keepdims=True)).astype(BF16)
        o = jnp.dot(w, vals, preferred_element_type=F32)
        out_ref[0, :, g * HD : (g + 1) * HD] = jnp.where(live, o, 0.0).astype(BF16)


def attend_call(slot, length, q, tkv, vis):
    n, seg = q.shape[0], q.shape[1]
    return pl.pallas_call(
        attend_kernel,
        out_shape=(
            jax.ShapeDtypeStruct((n, seg, KB), BF16),
            jax.ShapeDtypeStruct((n, seg, KVW), BF16),
        ),
        grid_spec=pltpu.PrefetchScalarGridSpec(
            num_scalar_prefetch=2,
            grid=(n,),
            in_specs=[
                pl.BlockSpec((1, seg, KB), lambda r, s, l: (r, 0, 0)),
                pl.BlockSpec((1, seg, KVW), lambda r, s, l: (r, 0, 0)),
                pl.BlockSpec((1, VIS, KVW), lambda r, s, l: (s[r], 0, 0)),
            ],
            out_specs=(
                pl.BlockSpec((1, seg, KB), lambda r, s, l: (r, 0, 0)),
                pl.BlockSpec((1, seg, KVW), lambda r, s, l: (r, 0, 0)),
            ),
        ),
        name="attend",
    )(slot, length, q, tkv, vis)


def per_device(
    image_map, conv_weight, conv_bias, ln_gain, ln_bias, connector, connector_bias,
    norm_gain, q_weight, kv_weight, text_hidden, rollout_group, text_length,
):
    dp = lax.axis_index("dp")
    rollouts, seg = text_hidden.shape[0], text_hidden.shape[1]
    kv = (kv_weight.reshape(D, KVW).astype(F32) * norm_gain[:, None]).astype(BF16)
    own_gain = lax.dynamic_slice(norm_gain, (dp * WR,), (WR,))
    w = (q_weight.astype(F32) * own_gain[:, None]).astype(BF16)
    q, tkv, own, vis = gather_call(
        image_map.reshape(SIDE, SIDE, CL), conv_weight,
        conv_bias.reshape(1, CL), ln_gain.reshape(1, CL), ln_bias.reshape(1, CL),
        connector_bias.reshape(1, D), connector, w, kv,
        text_hidden.reshape(2, HALF, KB),
    )
    slot = (rollout_group % 2) * 16 + rollout_group // 2
    attended, cache = attend_call(
        slot, text_length, q.reshape(rollouts, seg, KB), tkv.reshape(rollouts, seg, KVW),
        vis.reshape(32, VIS, KVW),
    )
    return (
        attended,
        cache.reshape(rollouts, seg, 1, 2, HD),
        own.reshape(1, VIS, 1, 2, HD),
    )


def solution(mesh):
    in_specs = (
        P("dp", None, None, "mp"),
        P(None, None, "mp"),
        P("mp"),
        P("mp"),
        P("mp"),
        P("mp", None),
        P(),
        P(),
        P("dp", "mp"),
        P(None, "mp", None, None),
        P("dp", None, "mp"),
        P("dp"),
        P("dp"),
    )
    out_specs = (
        P("dp", None, "mp"),
        P("dp", None, "mp", None, None),
        P("dp", None, "mp", None, None),
    )
    return jax.shard_map(
        per_device, mesh=mesh, in_specs=in_specs, out_specs=out_specs, check_vma=False
    )
```

```python
import functools

import jax
import jax.numpy as jnp
from jax import lax
from jax.experimental import pallas as pl
from jax.experimental.pallas import tpu as pltpu
from jax.sharding import PartitionSpec as P

MESH = pl.DeviceIdType.MESH
F32 = jnp.float32
BF16 = jnp.bfloat16

D = 7168
C = 3072
HD = 128
KSZ = 7
GQ = 7
SIDE = 16
VIS = 64
KB = 896
ROWS = 768
HALF = 384
QUART = 192
EIGHTH = 96
WR = 224
KVW = 256
CL = 384

A_L, A_R, A_Z, B_L, B_R, C_L, C_R, D_Z = range(8)


def gather_kernel(
    img, cw, cb, lg, lb, cbias, gain, conn_hbm, w_hbm, kv_hbm, x_hbm,
    q_out, tkv_out, own_out, vis_out,
    xraw, xbuf, wbuf, kvraw, kvbuf, connbuf, pad, conv, stats, ssb, part, rsb, pair, agb, qacc, kvacc,
    loc, x_s, x_r, w1_s, w1_r, w2_s, w2_r, wc_s, wc_r, st_s, st_r, ss_s, ss_r,
    rs_s, rs_r, ag_s, ag_r, v_s, v_r,
):
    dp = lax.axis_index("dp")
    mp = lax.axis_index("mp")
    y, zh, c = dp // 8, (dp // 2) % 4, dp % 2
    zl, x = mp // 4, mp % 4
    other = 1 - zl

    def mp_id(xx, zz):
        return zz * 4 + (xx + 4) % 4

    def dp_id(yy, zz, cc):
        return ((yy + 4) % 4) * 8 + ((zz + 4) % 4) * 2 + cc

    right, left, cross = (dp, mp_id(x + 1, zl)), (dp, mp_id(x - 1, zl)), (dp, mp_id(x, other))
    z_peer = [(dp_id(y, zh + d, c), mp) for d in (1, 2, 3)]
    y_peer = [(dp_id(y + d, zh, c), mp) for d in (1, 2, 3)]
    sib = (dp_id(y, zh, 1 - c), mp)
    mp_peer = [(dp, (mp + d) % 8) for d in range(1, 8)]

    def rcopy(src, dst, s, r, dev):
        return pltpu.make_async_remote_copy(src, dst, s, r, device_id=dev, device_id_type=MESH)

    bar = pltpu.get_barrier_semaphore()
    peers = mp_peer + z_peer + y_peer + [sib]
    for dev in peers:
        pl.semaphore_signal(bar, inc=1, device_id=dev, device_id_type=MESH)

    lc_x = pltpu.make_async_copy(x_hbm, xraw, loc.at[0])
    lc_w = pltpu.make_async_copy(w_hbm, wbuf.at[dp], loc.at[1])
    lc_kv = pltpu.make_async_copy(kv_hbm, kvraw, loc.at[2])
    lc_cn = pltpu.make_async_copy(conn_hbm, connbuf, loc.at[3])
    for cp in (lc_x, lc_w, lc_cn, lc_kv):
        cp.start()

    def gain_of(k):
        return gain[:, pl.ds(pl.multiple_of(k * KB, 128), KB)]

    lc_x.wait()
    for h in range(4):
        xbuf[mp, h] = (xraw[h].astype(F32) * gain_of(mp)).astype(BF16)

    pl.semaphore_wait(bar, len(peers))

    sends = []

    def go(cp):
        cp.start()
        sends.append(cp)

    def xcopy(h, slot, k, r0, rn, dev):
        piece = xbuf.at[k, h, pl.ds(r0, rn)]
        return rcopy(piece, piece, x_s.at[h, slot], x_r.at[h, slot], dev)

    def xsend(h, slot, k, r0, rn, dev):
        go(xcopy(h, slot, k, r0, rn, dev))

    def xrecv(h, slot, k, r0, rn):
        xcopy(h, slot, k, r0, rn, left).wait_recv()

    kl, kr, k2 = mp_id(x - 1, zl), mp_id(x + 1, zl), mp_id(x + 2, zl)
    kz, klz, krz, k2z = mp_id(x, other), mp_id(x - 1, other), mp_id(x + 1, other), mp_id(x + 2, other)

    x_peer = [(dp, mp_id(x + d, zl)) for d in (1, 2, 3)]

    def send_a(h):
        xsend(h, A_L, mp, 0, QUART, right)
        xsend(h, A_R, mp, 0, QUART, left)

    def send_az(h):
        xsend(h, A_Z, mp, 0, QUART, cross)

    def forward_b(h):
        xrecv(h, A_L, kl, 0, QUART)
        xsend(h, B_L, kl, 0, EIGHTH, right)
        xrecv(h, A_R, kr, 0, QUART)
        xsend(h, B_R, kr, EIGHTH, EIGHTH, left)

    def forward_c(h):
        xrecv(h, A_Z, kz, 0, QUART)
        xsend(h, C_L, kz, 0, QUART, right)
        xsend(h, C_R, kz, 0, QUART, left)

    def forward_d(h):
        xrecv(h, B_L, k2, 0, EIGHTH)
        xrecv(h, B_R, k2, EIGHTH, EIGHTH)
        xsend(h, D_Z, k2, 0, QUART, cross)

    def last_x(h):
        xrecv(h, C_L, klz, 0, QUART)
        xrecv(h, C_R, krz, 0, QUART)
        xrecv(h, D_Z, k2z, 0, QUART)

    def wslot(i):
        return wbuf.at[i]

    def wsend(src, i, s, r, dev):
        go(rcopy(src, wslot(i), s, r, dev))

    def wrecv(i, s, r):
        rcopy(wslot(i), wslot(i), s, r, sib).wait_recv()

    def half_w(i, p):
        return wbuf.at[i, pl.ds(p * (WR // 2), WR // 2)]

    zup, zdown = z_peer[0], z_peer[2]
    i_up, i_down, i_far = dp_id(y, zh + 1, c), dp_id(y, zh - 1, c), dp_id(y, zh + 2, c)
    wsend(w_hbm, dp, w1_s.at[0], w1_r.at[0], zup)
    wsend(w_hbm, dp, w1_s.at[1], w1_r.at[1], zdown)
    send_a(0)
    send_a(1)
    for d in range(3):
        wsend(w_hbm, dp, w2_s.at[0, d], w2_r.at[0, d], y_peer[d])
    wsend(w_hbm, dp, wc_s.at[0, 0], wc_r.at[0, 0], sib)

    pad[...] = jnp.zeros_like(pad)
    pad[3:19, 8:24, :] = img[...].astype(F32)

    def conv_lanes(l, carry):
        lanes = pl.ds(pl.multiple_of(l * 128, 128), 128)
        acc = jnp.zeros((SIDE, SIDE, 128), F32)
        taps = cw[:, :, lanes].astype(F32)
        for j in range(KSZ):
            cols = pad[:, 5 + j : 21 + j, lanes]
            for i in range(KSZ):
                acc = acc + cols[i : i + SIDE] * taps[i, j : j + 1].reshape(1, 1, 128)
        conv[:, lanes] = acc.reshape(SIDE * SIDE, 128)
        return carry

    lax.fori_loop(0, CL // 128, conv_lanes, 0)
    hi = lax.Precision.HIGHEST
    nt = (((1,), (1,)), ((), ()))
    ones = jnp.ones((8, CL), F32)
    cv = conv[...] + cb[...].reshape(1, CL)
    conv[...] = cv
    s1 = lax.dot_general(ones, cv, nt, precision=hi, preferred_element_type=F32)
    s2 = lax.dot_general(ones, cv * cv, nt, precision=hi, preferred_element_type=F32)
    stats[mp, 0:8] = s1
    stats[mp, 8:16] = s2
    for d in range(7):
        go(rcopy(stats.at[mp], stats.at[mp], st_s.at[d], st_r.at[d], mp_peer[d]))
    send_az(0)
    send_az(1)
    send_a(2)
    send_a(3)

    ones_b = jnp.ones((8, KB), BF16)
    for h in range(2):
        xv = xraw[2 * h : 2 * h + 2].reshape(HALF, KB).astype(F32)
        sq = xv * xv
        sq_hi = sq.astype(BF16)
        sq_lo = (sq - sq_hi.astype(F32)).astype(BF16)
        ssb[mp, :, h * HALF : (h + 1) * HALF] = lax.dot_general(
            ones_b, sq_hi, nt, preferred_element_type=F32
        ) + lax.dot_general(ones_b, sq_lo, nt, preferred_element_type=F32)
    for d in range(7):
        go(rcopy(ssb.at[mp], ssb.at[mp], ss_s.at[d], ss_r.at[d], mp_peer[d]))

    def src_of(d):
        return (mp + 7 - d) % 8

    def spread_w(e, i):
        for d in range(3):
            wsend(wslot(i), i, w2_s.at[e, d], w2_r.at[e, d], y_peer[d])
        wsend(wslot(i), i, wc_s.at[e, 0], wc_r.at[e, 0], sib)

    wrecv(i_down, w1_s.at[0], w1_r.at[0])
    go(rcopy(half_w(i_down, 0), half_w(i_down, 0), w1_s.at[2], w1_r.at[2], zup))
    spread_w(1, i_down)
    wrecv(i_up, w1_s.at[1], w1_r.at[1])
    go(rcopy(half_w(i_up, 1), half_w(i_up, 1), w1_s.at[3], w1_r.at[3], zdown))
    spread_w(2, i_up)
    send_az(2)
    send_az(3)
    forward_b(0)
    forward_b(1)

    for d in range(7):
        sd = src_of(d)
        rcopy(stats.at[sd], stats.at[sd], st_s.at[d], st_r.at[d], sib).wait_recv()
    tot = stats[0]
    for k in range(1, 8):
        tot = tot + stats[k]
    avg = tot[0:1] * (1.0 / C)
    var = tot[8:9] * (1.0 / C) - avg * avg
    rstd = lax.rsqrt(var + 1e-06)
    vrow = lax.broadcasted_iota(jnp.int32, (VIS, SIDE * SIDE), 0)
    pix = lax.broadcasted_iota(jnp.int32, (VIS, SIDE * SIDE), 1)
    hit = (vrow // 8 == pix // 32) & (vrow % 8 == (pix % 16) // 2)
    pool = jnp.where(hit, 0.25 * rstd, 0.0)
    shift = jnp.sum(pool * avg, axis=1, keepdims=True)
    mixed = jnp.dot(pool, conv[...], precision=hi, preferred_element_type=F32)
    pooled = ((mixed - shift) * lg[...].reshape(1, CL) + lb[...].reshape(1, CL)).astype(BF16)
    lc_cn.wait()

    def project(j):
        cols = pl.ds(pl.multiple_of(j * KB, 128), KB)
        return jnp.dot(pooled, connbuf[:, cols], preferred_element_type=F32)

    def pair_of(xx):
        own = project(mp_id(xx, zl))
        far = project(mp_id(xx, other))
        return own, far

    for d in range(3):
        own_p, far_p = pair_of(x + d + 1)
        xx = (x + d + 1) % 4
        part[xx, 0] = own_p.astype(BF16)
        part[xx, 1] = far_p.astype(BF16)
        go(rcopy(part.at[xx], rsb.at[x], rs_s.at[d], rs_r.at[d], x_peer[d]))
    near_sum, far_sum = pair_of(x)

    rcopy(half_w(i_far, 0), half_w(i_far, 0), w1_s.at[2], w1_r.at[2], sib).wait_recv()
    rcopy(half_w(i_far, 1), half_w(i_far, 1), w1_s.at[3], w1_r.at[3], sib).wait_recv()
    spread_w(3, i_far)
    forward_b(2)
    forward_b(3)
    forward_c(0)

    lc_kv.wait()

    def kv_flat(n, carry):
        rows = pl.ds(n * 256, 256)
        kvbuf[rows] = kvraw[rows].reshape(256, KVW)
        return carry

    lax.fori_loop(0, D // 256, kv_flat, 0)
    kvacc[...] = jnp.zeros_like(kvacc)
    qacc[...] = jnp.zeros_like(qacc)

    def x_half(h, k):
        return xbuf[k, pl.ds(h * 2, 2)].reshape(HALF, KB)

    def kv_unit(h, k):
        kvacc[h] += jnp.dot(x_half(h, k), kvbuf[pl.ds(k * KB, KB)], preferred_element_type=F32)

    def q_unit(h, k):
        w = wbuf[pl.ds(k * 4, 4)].reshape(KB, KB)
        qacc[h] += jnp.dot(x_half(h, k), w, preferred_element_type=F32)

    def each(fn, ks):
        def step(n, carry):
            h, m = n // len(ks), n % len(ks)
            k = ks[0]
            for t in range(1, len(ks)):
                k = jnp.where(m == t, ks[t], k)
            fn(h, k)
            return carry

        lax.fori_loop(0, 2 * len(ks), step, 0)

    each(kv_unit, [mp, kl, kr])

    def from_x(d):
        return (x + 3 - d) % 4

    for d in range(3):
        sx = from_x(d)
        rcopy(rsb.at[sx], rsb.at[sx], rs_s.at[d], rs_r.at[d], sib).wait_recv()
        near_sum = near_sum + rsb[sx, 0].astype(F32)
        far_sum = far_sum + rsb[sx, 1].astype(F32)
    pair[0] = far_sum.astype(BF16)
    go(rcopy(pair.at[0], pair.at[1], rs_s.at[3], rs_r.at[3], cross))
    rcopy(pair.at[0], pair.at[1], rs_s.at[3], rs_r.at[3], cross).wait_recv()
    summed = near_sum + pair[1].astype(F32) + cbias[:, pl.ds(pl.multiple_of(mp * KB, 128), KB)]
    agb[x, zl] = summed.astype(BF16)
    go(rcopy(agb.at[x, zl], agb.at[x, zl], ag_s.at[3], ag_r.at[3], cross))
    forward_d(0)
    forward_d(1)
    rcopy(agb.at[x, other], agb.at[x, other], ag_s.at[3], ag_r.at[3], cross).wait_recv()
    for d in range(3):
        go(rcopy(agb.at[x], agb.at[x], ag_s.at[d], ag_r.at[d], x_peer[d]))

    forward_c(1)
    forward_c(2)
    forward_c(3)
    each(kv_unit, [kz])

    i_of = [dp, i_down, i_up, i_far]

    def at_y(i, d):
        return (i + 32 - 8 * d) % 32

    def hand_w(e):
        for d in range(3):
            i = at_y(i_of[e], d + 1)
            wrecv(i, w2_s.at[e, d], w2_r.at[e, d])
            wsend(wslot(i), i, wc_s.at[e, d + 1], wc_r.at[e, d + 1], sib)

    for e in range(3):
        hand_w(e)

    for d in range(3):
        sx = from_x(d)
        rcopy(agb.at[sx], agb.at[sx], ag_s.at[d], ag_r.at[d], sib).wait_recv()

    def vis_step(k, carry):
        acc, sq = carry
        vf = agb[k % 4, k // 4].astype(F32)
        sq = sq + jnp.sum(vf * vf, axis=1, keepdims=True)
        vg = (vf * gain_of(k)).astype(BF16)
        acc = acc + jnp.dot(vg, kvbuf[pl.ds(k * KB, KB)], preferred_element_type=F32)
        return acc, sq

    vacc, vsq = lax.fori_loop(0, 8, vis_step, (jnp.zeros((VIS, KVW), F32), jnp.zeros((VIS, 1), F32)))
    vkv = (vacc * lax.rsqrt(vsq * (1.0 / D) + 1e-05)).astype(BF16)
    own_out[...] = vkv
    vis_out[c, y, zh] = vkv
    for d in range(3):
        piece = vis_out.at[c, y, zh]
        go(rcopy(piece, piece, v_s.at[d], v_r.at[d], z_peer[d]))

    forward_d(2)
    forward_d(3)
    hand_w(3)
    for e in range(4):
        for d in range(4):
            i = at_y((i_of[e] // 2) * 2 + 1 - c, d)
            wrecv(i, wc_s.at[e, d], wc_r.at[e, d])
    lc_w.wait()

    each(kv_unit, [k2])
    each(q_unit, [mp, kl, kr, k2, kz])

    for d in range(3):
        piece = vis_out.at[c, y, (zh + 3 - d) % 4]
        rcopy(piece, piece, v_s.at[d], v_r.at[d], sib).wait_recv()
    for d in range(3):
        piece = vis_out.at[c, y]
        go(rcopy(piece, piece, v_s.at[3 + d], v_r.at[3 + d], y_peer[d]))

    def unit(h, k):
        kv_unit(h, k)
        q_unit(h, k)

    last_x(0)
    last_x(1)

    def unit_h(h):
        def step(n, carry):
            unit(h, jnp.where(n == 0, klz, jnp.where(n == 1, krz, k2z)))
            return carry
        lax.fori_loop(0, 3, step, 0)
    unit_h(0)

    for d in range(3):
        piece = vis_out.at[c, (y + 3 - d) % 4]
        rcopy(piece, piece, v_s.at[3 + d], v_r.at[3 + d], sib).wait_recv()
    go(rcopy(vis_out.at[c], vis_out.at[c], v_s.at[6], v_r.at[6], sib))

    for d in range(7):
        sd = src_of(d)
        rcopy(ssb.at[sd], ssb.at[sd], ss_s.at[d], ss_r.at[d], sib).wait_recv()
    ss = ssb[0]
    for k in range(1, 8):
        ss = ss + ssb[k]
    inv = lax.rsqrt(ss * (1.0 / D) + 1e-05)
    inv = jnp.transpose(jnp.broadcast_to(inv[0:1], (128, ROWS)))

    def finish(h):
        scale = inv[h * HALF : (h + 1) * HALF, 0:1]
        q_out[h] = (qacc[h] * scale).astype(BF16)
        tkv_out[h] = (kvacc[h] * scale).astype(BF16)

    finish(0)
    last_x(2)
    last_x(3)
    unit_h(1)
    finish(1)

    rcopy(vis_out.at[1 - c], vis_out.at[1 - c], v_s.at[6], v_r.at[6], sib).wait_recv()
    for cp in sends:
        cp.wait_send()


def gather_call(img, cw, cb, lg, lb, cbias, gain, conn, w, kv, text):
    vm = pl.BlockSpec(memory_space=pltpu.VMEM)
    hb = pl.BlockSpec(memory_space=pl.ANY)
    dma = pltpu.SemaphoreType.DMA
    return pl.pallas_call(
        gather_kernel,
        out_shape=(
            jax.ShapeDtypeStruct((2, HALF, KB), BF16),
            jax.ShapeDtypeStruct((2, HALF, KVW), BF16),
            jax.ShapeDtypeStruct((VIS, KVW), BF16),
            jax.ShapeDtypeStruct((2, 4, 4, VIS, KVW), BF16),
        ),
        in_specs=[vm] * 7 + [hb] * 4,
        out_specs=(vm,) * 4,
        scratch_shapes=[
            pltpu.VMEM((4, QUART, KB), BF16),
            pltpu.VMEM((8, 4, QUART, KB), BF16),
            pltpu.VMEM((32, WR, KB), BF16),
            pltpu.VMEM((D, 2, HD), BF16),
            pltpu.VMEM((D, KVW), BF16),
            pltpu.VMEM((CL, D), BF16),
            pltpu.VMEM((22, 32, CL), F32),
            pltpu.VMEM((SIDE * SIDE, CL), F32),
            pltpu.VMEM((8, 16, SIDE * SIDE), F32),
            pltpu.VMEM((8, 8, ROWS), F32),
            pltpu.VMEM((4, 2, VIS, KB), BF16),
            pltpu.VMEM((4, 2, VIS, KB), BF16),
            pltpu.VMEM((2, VIS, KB), BF16),
            pltpu.VMEM((4, 2, VIS, KB), BF16),
            pltpu.VMEM((2, HALF, KB), F32),
            pltpu.VMEM((2, HALF, KVW), F32),
            dma((4,)),
            dma((4, 8)), dma((4, 8)),
            dma((4,)), dma((4,)),
            dma((4, 3)), dma((4, 3)),
            dma((4, 4)), dma((4, 4)),
            dma((7,)), dma((7,)),
            dma((7,)), dma((7,)),
            dma((4,)), dma((4,)),
            dma((4,)), dma((4,)),
            dma((7,)), dma((7,)),
        ],
        compiler_params=pltpu.CompilerParams(
            collective_id=0, has_side_effects=True, vmem_limit_bytes=58 * 2**20
        ),
        cost_estimate=pl.CostEstimate(
            flops=14 * 10**9, bytes_accessed=30 * 10**6, transcendentals=0
        ),
        name="gather",
    )(img, cw, cb, lg, lb, cbias, gain, conn, w, kv, text)


def attend_kernel(group, length, q_ref, t_ref, v_ref, own_ref, out_ref, cache_ref, vis_ref):
    n = length[pl.program_id(0)]
    seg = q_ref.shape[1]
    live = lax.broadcasted_iota(jnp.int32, (seg, 1), 0) < n
    text = jnp.where(live, t_ref[0].astype(F32), 0.0).astype(BF16)
    cache_ref[0] = text.reshape(seg, 2, HD)

    @pl.when(pl.program_id(0) == 0)
    def _():
        vis_ref[...] = own_ref[...].reshape(VIS, 2, HD)

    vis = v_ref[0]
    nt = (((1,), (1,)), ((), ()))
    q = jnp.concatenate([q_ref[0, :, g * HD : (g + 1) * HD] for g in range(GQ)], axis=0)
    rows = GQ * seg
    qi = lax.broadcasted_iota(jnp.int32, (rows, seg), 0) % seg
    ki = lax.broadcasted_iota(jnp.int32, (rows, seg), 1)
    scale = HD ** (-0.5)
    st = lax.dot_general(q, text[:, :HD], nt, preferred_element_type=F32)
    sv = lax.dot_general(q, vis[:, :HD], nt, preferred_element_type=F32)
    st = jnp.where(ki <= qi, st, -1e30)
    peak = jnp.maximum(jnp.max(st, axis=-1, keepdims=True), jnp.max(sv, axis=-1, keepdims=True))
    et = jnp.exp((st - peak) * scale)
    ev = jnp.exp((sv - peak) * scale)
    over = 1.0 / (jnp.sum(et, axis=-1, keepdims=True) + jnp.sum(ev, axis=-1, keepdims=True))
    o = jnp.dot((et * over).astype(BF16), text[:, HD:], preferred_element_type=F32)
    o = o + jnp.dot((ev * over).astype(BF16), vis[:, HD:], preferred_element_type=F32)
    for g in range(GQ):
        out_ref[0, :, g * HD : (g + 1) * HD] = jnp.where(
            live, o[g * seg : (g + 1) * seg], 0.0
        ).astype(BF16)


def attend_call(group, length, q, tkv, vis, own):
    n, seg = q.shape[0], q.shape[1]
    return pl.pallas_call(
        attend_kernel,
        out_shape=(
            jax.ShapeDtypeStruct((n, seg, KB), BF16),
            jax.ShapeDtypeStruct((n, seg, 2, HD), BF16),
            jax.ShapeDtypeStruct((VIS, 2, HD), BF16),
        ),
        grid_spec=pltpu.PrefetchScalarGridSpec(
            num_scalar_prefetch=2,
            grid=(n,),
            in_specs=[
                pl.BlockSpec((1, seg, KB), lambda r, s, l: (r, 0, 0)),
                pl.BlockSpec((1, seg, KVW), lambda r, s, l: (r, 0, 0)),
                pl.BlockSpec((1, VIS, KVW), lambda r, s, l: (s[r] % 2 * 16 + s[r] // 2, 0, 0)),
                pl.BlockSpec((VIS, KVW), lambda r, s, l: (0, 0)),
            ],
            out_specs=(
                pl.BlockSpec((1, seg, KB), lambda r, s, l: (r, 0, 0)),
                pl.BlockSpec((1, seg, 2, HD), lambda r, s, l: (r, 0, 0, 0)),
                pl.BlockSpec((VIS, 2, HD), lambda r, s, l: (0, 0, 0)),
            ),
        ),
        name="attend",
    )(group, length, q, tkv, vis, own)


def per_device(
    image_map, conv_weight, conv_bias, ln_gain, ln_bias, connector, connector_bias,
    norm_gain, q_weight, kv_weight, text_hidden, rollout_group, text_length,
):
    rollouts, seg = text_hidden.shape[0], text_hidden.shape[1]
    q, tkv, own, vis = gather_call(
        image_map.reshape(SIDE, SIDE, CL), conv_weight,
        conv_bias, ln_gain, ln_bias,
        connector_bias.reshape(1, D), norm_gain.reshape(1, D), connector, q_weight,
        kv_weight.reshape(D, 2, HD), text_hidden.reshape(4, QUART, KB),
    )
    attended, cache, own = attend_call(
        rollout_group, text_length, q.reshape(rollouts, seg, KB), tkv.reshape(rollouts, seg, KVW),
        vis.reshape(32, VIS, KVW), own,
    )
    return (
        attended,
        cache.reshape(rollouts, seg, 1, 2, HD),
        own.reshape(1, VIS, 1, 2, HD),
    )


def solution(mesh):
    in_specs = (
        P("dp", None, None, "mp"),
        P(None, None, "mp"),
        P("mp"),
        P("mp"),
        P("mp"),
        P("mp", None),
        P(),
        P(),
        P("dp", "mp"),
        P(None, "mp", None, None),
        P("dp", None, "mp"),
        P("dp"),
        P("dp"),
    )
    out_specs = (
        P("dp", None, "mp"),
        P("dp", None, "mp", None, None),
        P("dp", None, "mp", None, None),
    )
    return jax.shard_map(
        per_device, mesh=mesh, in_specs=in_specs, out_specs=out_specs, check_vma=False
    )
```

```python
import functools

import jax
import jax.numpy as jnp
from jax import lax
from jax.experimental import pallas as pl
from jax.experimental.pallas import tpu as pltpu
from jax.sharding import PartitionSpec as P

MESH = pl.DeviceIdType.MESH
F32 = jnp.float32
BF16 = jnp.bfloat16

D = 7168
C = 3072
HD = 128
KSZ = 7
GQ = 7
SIDE = 16
VIS = 64
KB = 896
ROWS = 768
HALF = 384
QUART = 192
EIGHTH = 96
LOG2E = 1.4426950408889634
WR = 224
KVW = 256
CL = 384

A_L, A_R, A_Z, B_L, B_R, C_L, C_R, D_Z = range(8)


def gather_kernel(
    img, cw, cb, lg, lb, cbias, gain, conn_hbm, w_hbm, kv_hbm, x_hbm,
    q_out, tkv_out, own_out, vis_out,
    xraw, xbuf, wbuf, kvraw, kvbuf, connbuf, pad, conv, stats, ssb, part, rsb, pair, agb, qacc, kvacc,
    loc, x_s, x_r, w1_s, w1_r, w2_s, w2_r, wc_s, wc_r, st_s, st_r, ss_s, ss_r,
    rs_s, rs_r, ag_s, ag_r, v_s, v_r,
):
    dp = lax.axis_index("dp")
    mp = lax.axis_index("mp")
    y, zh, c = dp // 8, (dp // 2) % 4, dp % 2
    zl, x = mp // 4, mp % 4
    other = 1 - zl

    def mp_id(xx, zz):
        return zz * 4 + (xx + 4) % 4

    def dp_id(yy, zz, cc):
        return ((yy + 4) % 4) * 8 + ((zz + 4) % 4) * 2 + cc

    right, left, cross = (dp, mp_id(x + 1, zl)), (dp, mp_id(x - 1, zl)), (dp, mp_id(x, other))
    z_peer = [(dp_id(y, zh + d, c), mp) for d in (1, 2, 3)]
    y_peer = [(dp_id(y + d, zh, c), mp) for d in (1, 2, 3)]
    sib = (dp_id(y, zh, 1 - c), mp)
    mp_peer = [(dp, (mp + d) % 8) for d in range(1, 8)]

    def rcopy(src, dst, s, r, dev):
        return pltpu.make_async_remote_copy(src, dst, s, r, device_id=dev, device_id_type=MESH)

    bar = pltpu.get_barrier_semaphore()
    peers = mp_peer + z_peer + y_peer + [sib]
    for dev in peers:
        pl.semaphore_signal(bar, inc=1, device_id=dev, device_id_type=MESH)

    lc_x = pltpu.make_async_copy(x_hbm, xraw, loc.at[0])
    lc_w = pltpu.make_async_copy(w_hbm, wbuf.at[dp], loc.at[1])
    lc_kv = pltpu.make_async_copy(kv_hbm, kvraw, loc.at[2])
    lc_cn = pltpu.make_async_copy(conn_hbm, connbuf, loc.at[3])
    for cp in (lc_x, lc_w, lc_cn, lc_kv):
        cp.start()

    def gain_of(k):
        return gain[:, pl.ds(pl.multiple_of(k * KB, 128), KB)]

    lc_x.wait()
    for h in range(4):
        xbuf[mp, h] = (xraw[h].astype(F32) * gain_of(mp)).astype(BF16)

    pl.semaphore_wait(bar, len(peers))

    sends = []

    def go(cp):
        cp.start()
        sends.append(cp)

    def xcopy(h, slot, k, r0, rn, dev):
        piece = xbuf.at[k, h, pl.ds(r0, rn)]
        return rcopy(piece, piece, x_s.at[h, slot], x_r.at[h, slot], dev)

    def xsend(h, slot, k, r0, rn, dev):
        go(xcopy(h, slot, k, r0, rn, dev))

    def xrecv(h, slot, k, r0, rn):
        xcopy(h, slot, k, r0, rn, left).wait_recv()

    kl, kr, k2 = mp_id(x - 1, zl), mp_id(x + 1, zl), mp_id(x + 2, zl)
    kz, klz, krz, k2z = mp_id(x, other), mp_id(x - 1, other), mp_id(x + 1, other), mp_id(x + 2, other)

    x_peer = [(dp, mp_id(x + d, zl)) for d in (1, 2, 3)]

    def send_a(h):
        xsend(h, A_L, mp, 0, QUART, right)
        xsend(h, A_R, mp, 0, QUART, left)

    def send_az(h):
        xsend(h, A_Z, mp, 0, QUART, cross)

    def forward_b(h):
        xrecv(h, A_L, kl, 0, QUART)
        xsend(h, B_L, kl, 0, EIGHTH, right)
        xrecv(h, A_R, kr, 0, QUART)
        xsend(h, B_R, kr, EIGHTH, EIGHTH, left)

    def forward_c(h):
        xrecv(h, A_Z, kz, 0, QUART)
        xsend(h, C_L, kz, 0, QUART, right)
        xsend(h, C_R, kz, 0, QUART, left)

    def forward_d(h):
        xrecv(h, B_L, k2, 0, EIGHTH)
        xrecv(h, B_R, k2, EIGHTH, EIGHTH)
        xsend(h, D_Z, k2, 0, QUART, cross)

    def last_x(h):
        xrecv(h, C_L, klz, 0, QUART)
        xrecv(h, C_R, krz, 0, QUART)
        xrecv(h, D_Z, k2z, 0, QUART)

    def wslot(i):
        return wbuf.at[i]

    def wsend(src, i, s, r, dev):
        go(rcopy(src, wslot(i), s, r, dev))

    def wrecv(i, s, r):
        rcopy(wslot(i), wslot(i), s, r, sib).wait_recv()

    def half_w(i, p):
        return wbuf.at[i, pl.ds(p * (WR // 2), WR // 2)]

    zup, zdown = z_peer[0], z_peer[2]
    i_up, i_down, i_far = dp_id(y, zh + 1, c), dp_id(y, zh - 1, c), dp_id(y, zh + 2, c)
    wsend(w_hbm, dp, w1_s.at[0], w1_r.at[0], zup)
    wsend(w_hbm, dp, w1_s.at[1], w1_r.at[1], zdown)
    send_a(0)
    send_a(1)
    for d in range(3):
        wsend(w_hbm, dp, w2_s.at[0, d], w2_r.at[0, d], y_peer[d])
    wsend(w_hbm, dp, wc_s.at[0, 0], wc_r.at[0, 0], sib)

    pad[...] = jnp.zeros_like(pad)
    pad[3:19, 8:24, :] = img[...].astype(F32)

    def conv_lanes(l, carry):
        lanes = pl.ds(pl.multiple_of(l * 128, 128), 128)
        acc = jnp.zeros((SIDE, SIDE, 128), F32)
        taps = cw[:, :, lanes].astype(F32)
        for j in range(KSZ):
            cols = pad[:, 5 + j : 21 + j, lanes]
            for i in range(KSZ):
                acc = acc + cols[i : i + SIDE] * taps[i, j : j + 1].reshape(1, 1, 128)
        conv[:, lanes] = acc.reshape(SIDE * SIDE, 128)
        return carry

    lax.fori_loop(0, CL // 128, conv_lanes, 0)
    hi = lax.Precision.HIGHEST
    nt = (((1,), (1,)), ((), ()))
    ones = jnp.ones((8, CL), F32)
    cv = conv[...] + cb[...].reshape(1, CL)
    conv[...] = cv
    s1 = lax.dot_general(ones, cv, nt, precision=hi, preferred_element_type=F32)
    s2 = lax.dot_general(ones, cv * cv, nt, precision=hi, preferred_element_type=F32)
    stats[mp, 0:8] = s1
    stats[mp, 8:16] = s2
    for d in range(7):
        go(rcopy(stats.at[mp], stats.at[mp], st_s.at[d], st_r.at[d], mp_peer[d]))
    send_az(0)
    send_az(1)
    send_a(2)
    send_a(3)

    ones_b = jnp.ones((8, KB), BF16)
    for h in range(2):
        xv = xraw[2 * h : 2 * h + 2].reshape(HALF, KB).astype(F32)
        sq = xv * xv
        sq_hi = sq.astype(BF16)
        sq_lo = (sq - sq_hi.astype(F32)).astype(BF16)
        ssb[mp, :, h * HALF : (h + 1) * HALF] = lax.dot_general(
            ones_b, sq_hi, nt, preferred_element_type=F32
        ) + lax.dot_general(ones_b, sq_lo, nt, preferred_element_type=F32)
    for d in range(7):
        go(rcopy(ssb.at[mp], ssb.at[mp], ss_s.at[d], ss_r.at[d], mp_peer[d]))

    def src_of(d):
        return (mp + 7 - d) % 8

    def spread_w(e, i):
        for d in range(3):
            wsend(wslot(i), i, w2_s.at[e, d], w2_r.at[e, d], y_peer[d])
        wsend(wslot(i), i, wc_s.at[e, 0], wc_r.at[e, 0], sib)

    wrecv(i_down, w1_s.at[0], w1_r.at[0])
    go(rcopy(half_w(i_down, 0), half_w(i_down, 0), w1_s.at[2], w1_r.at[2], zup))
    spread_w(1, i_down)
    wrecv(i_up, w1_s.at[1], w1_r.at[1])
    go(rcopy(half_w(i_up, 1), half_w(i_up, 1), w1_s.at[3], w1_r.at[3], zdown))
    spread_w(2, i_up)
    send_az(2)

    for d in range(7):
        sd = src_of(d)
        rcopy(stats.at[sd], stats.at[sd], st_s.at[d], st_r.at[d], sib).wait_recv()
    tot = stats[0]
    for k in range(1, 8):
        tot = tot + stats[k]
    avg = tot[0:1] * (1.0 / C)
    var = tot[8:9] * (1.0 / C) - avg * avg
    rstd = lax.rsqrt(var + 1e-06)
    vrow = lax.broadcasted_iota(jnp.int32, (VIS, SIDE * SIDE), 0)
    pix = lax.broadcasted_iota(jnp.int32, (VIS, SIDE * SIDE), 1)
    hit = (vrow // 8 == pix // 32) & (vrow % 8 == (pix % 16) // 2)
    pool = jnp.where(hit, 0.25 * rstd, 0.0)
    shift = jnp.sum(pool * avg, axis=1, keepdims=True)
    mixed = jnp.dot(pool, conv[...], precision=hi, preferred_element_type=F32)
    pooled = ((mixed - shift) * lg[...].reshape(1, CL) + lb[...].reshape(1, CL)).astype(BF16)
    lc_cn.wait()

    def project(j):
        cols = pl.ds(pl.multiple_of(j * KB, 128), KB)
        return jnp.dot(pooled, connbuf[:, cols], preferred_element_type=F32)

    def pair_of(xx):
        own = project(mp_id(xx, zl))
        far = project(mp_id(xx, other))
        return own, far

    for d in range(3):
        own_p, far_p = pair_of(x + d + 1)
        xx = (x + d + 1) % 4
        part[xx, 0] = own_p.astype(BF16)
        part[xx, 1] = far_p.astype(BF16)
        go(rcopy(part.at[xx], rsb.at[x], rs_s.at[d], rs_r.at[d], x_peer[d]))
    near_sum, far_sum = pair_of(x)

    rcopy(half_w(i_far, 0), half_w(i_far, 0), w1_s.at[2], w1_r.at[2], sib).wait_recv()
    rcopy(half_w(i_far, 1), half_w(i_far, 1), w1_s.at[3], w1_r.at[3], sib).wait_recv()
    spread_w(3, i_far)
    forward_b(0)
    forward_b(1)
    forward_b(2)
    forward_b(3)

    lc_kv.wait()

    def kv_flat(n, carry):
        rows = pl.ds(n * 256, 256)
        kvbuf[rows] = kvraw[rows].reshape(256, KVW)
        return carry

    lax.fori_loop(0, D // 256, kv_flat, 0)
    kvacc[...] = jnp.zeros_like(kvacc)
    qacc[...] = jnp.zeros_like(qacc)

    def x_half(h, k):
        return xbuf[k, pl.ds(h * 2, 2)].reshape(HALF, KB)

    def kv_unit(h, k):
        kvacc[h] += jnp.dot(x_half(h, k), kvbuf[pl.ds(k * KB, KB)], preferred_element_type=F32)

    def q_unit(h, k):
        w = wbuf[pl.ds(k * 4, 4)].reshape(KB, KB)
        qacc[h] += jnp.dot(x_half(h, k), w, preferred_element_type=F32)

    def each(fn, ks):
        def step(n, carry):
            h, m = n // len(ks), n % len(ks)
            k = ks[0]
            for t in range(1, len(ks)):
                k = jnp.where(m == t, ks[t], k)
            fn(h, k)
            return carry

        lax.fori_loop(0, 2 * len(ks), step, 0)

    each(kv_unit, [mp, kl, kr])

    def from_x(d):
        return (x + 3 - d) % 4

    for d in range(3):
        sx = from_x(d)
        rcopy(rsb.at[sx], rsb.at[sx], rs_s.at[d], rs_r.at[d], sib).wait_recv()
        near_sum = near_sum + rsb[sx, 0].astype(F32)
        far_sum = far_sum + rsb[sx, 1].astype(F32)
    pair[0] = far_sum.astype(BF16)
    go(rcopy(pair.at[0], pair.at[1], rs_s.at[3], rs_r.at[3], cross))
    rcopy(pair.at[0], pair.at[1], rs_s.at[3], rs_r.at[3], cross).wait_recv()
    summed = near_sum + pair[1].astype(F32) + cbias[:, pl.ds(pl.multiple_of(mp * KB, 128), KB)]
    agb[x, zl] = summed.astype(BF16)
    go(rcopy(agb.at[x, zl], agb.at[x, zl], ag_s.at[3], ag_r.at[3], cross))
    send_az(3)
    forward_d(0)
    rcopy(agb.at[x, other], agb.at[x, other], ag_s.at[3], ag_r.at[3], cross).wait_recv()
    for d in range(3):
        go(rcopy(agb.at[x], agb.at[x], ag_s.at[d], ag_r.at[d], x_peer[d]))

    forward_c(0)
    forward_c(1)
    forward_c(2)
    forward_d(1)
    forward_c(3)
    each(kv_unit, [kz])

    i_of = [dp, i_down, i_up, i_far]

    def at_y(i, d):
        return (i + 32 - 8 * d) % 32

    def hand_w(e):
        for d in range(3):
            i = at_y(i_of[e], d + 1)
            wrecv(i, w2_s.at[e, d], w2_r.at[e, d])
            wsend(wslot(i), i, wc_s.at[e, d + 1], wc_r.at[e, d + 1], sib)

    for e in range(3):
        hand_w(e)

    for d in range(3):
        sx = from_x(d)
        rcopy(agb.at[sx], agb.at[sx], ag_s.at[d], ag_r.at[d], sib).wait_recv()

    def vis_step(k, carry):
        acc, sq = carry
        vf = agb[k % 4, k // 4].astype(F32)
        sq = sq + jnp.sum(vf * vf, axis=1, keepdims=True)
        vg = (vf * gain_of(k)).astype(BF16)
        acc = acc + jnp.dot(vg, kvbuf[pl.ds(k * KB, KB)], preferred_element_type=F32)
        return acc, sq

    vacc, vsq = lax.fori_loop(0, 8, vis_step, (jnp.zeros((VIS, KVW), F32), jnp.zeros((VIS, 1), F32)))
    vkv = (vacc * lax.rsqrt(vsq * (1.0 / D) + 1e-05)).astype(BF16)
    own_out[...] = vkv
    vis_out[c, y, zh] = vkv
    for d in range(3):
        piece = vis_out.at[c, y, zh]
        go(rcopy(piece, piece, v_s.at[d], v_r.at[d], z_peer[d]))

    forward_d(2)
    forward_d(3)
    hand_w(3)
    for e in range(4):
        for d in range(4):
            i = at_y((i_of[e] // 2) * 2 + 1 - c, d)
            wrecv(i, wc_s.at[e, d], wc_r.at[e, d])
    lc_w.wait()

    each(kv_unit, [k2])
    each(q_unit, [mp, kl, kr, k2, kz])

    for d in range(3):
        piece = vis_out.at[c, y, (zh + 3 - d) % 4]
        rcopy(piece, piece, v_s.at[d], v_r.at[d], sib).wait_recv()
    for d in range(3):
        piece = vis_out.at[c, y]
        go(rcopy(piece, piece, v_s.at[3 + d], v_r.at[3 + d], y_peer[d]))

    def unit(h, k):
        kv_unit(h, k)
        q_unit(h, k)

    last_x(0)
    last_x(1)

    def unit_h(h):
        def step(n, carry):
            unit(h, jnp.where(n == 0, klz, jnp.where(n == 1, krz, k2z)))
            return carry
        lax.fori_loop(0, 3, step, 0)
    unit_h(0)

    for d in range(3):
        piece = vis_out.at[c, (y + 3 - d) % 4]
        rcopy(piece, piece, v_s.at[3 + d], v_r.at[3 + d], sib).wait_recv()
    go(rcopy(vis_out.at[c], vis_out.at[c], v_s.at[6], v_r.at[6], sib))

    for d in range(7):
        sd = src_of(d)
        rcopy(ssb.at[sd], ssb.at[sd], ss_s.at[d], ss_r.at[d], sib).wait_recv()
    ss = ssb[0]
    for k in range(1, 8):
        ss = ss + ssb[k]
    inv = lax.rsqrt(ss * (1.0 / D) + 1e-05)
    inv = jnp.transpose(jnp.broadcast_to(inv[0:1], (128, ROWS)))

    def finish(h):
        scale = inv[h * HALF : (h + 1) * HALF, 0:1]
        q_out[h] = (qacc[h] * scale).astype(BF16)
        tkv_out[h] = (kvacc[h] * scale).astype(BF16)

    finish(0)
    last_x(2)
    last_x(3)
    unit_h(1)
    finish(1)

    rcopy(vis_out.at[1 - c], vis_out.at[1 - c], v_s.at[6], v_r.at[6], sib).wait_recv()
    for cp in sends:
        cp.wait_send()


def gather_call(img, cw, cb, lg, lb, cbias, gain, conn, w, kv, text):
    vm = pl.BlockSpec(memory_space=pltpu.VMEM)
    hb = pl.BlockSpec(memory_space=pl.ANY)
    dma = pltpu.SemaphoreType.DMA
    return pl.pallas_call(
        gather_kernel,
        out_shape=(
            jax.ShapeDtypeStruct((2, HALF, KB), BF16),
            jax.ShapeDtypeStruct((2, HALF, KVW), BF16),
            jax.ShapeDtypeStruct((VIS, KVW), BF16),
            jax.ShapeDtypeStruct((2, 4, 4, VIS, KVW), BF16),
        ),
        in_specs=[vm] * 7 + [hb] * 4,
        out_specs=(vm,) * 4,
        scratch_shapes=[
            pltpu.VMEM((4, QUART, KB), BF16),
            pltpu.VMEM((8, 4, QUART, KB), BF16),
            pltpu.VMEM((32, WR, KB), BF16),
            pltpu.VMEM((D, 2, HD), BF16),
            pltpu.VMEM((D, KVW), BF16),
            pltpu.VMEM((CL, D), BF16),
            pltpu.VMEM((22, 32, CL), F32),
            pltpu.VMEM((SIDE * SIDE, CL), F32),
            pltpu.VMEM((8, 16, SIDE * SIDE), F32),
            pltpu.VMEM((8, 8, ROWS), F32),
            pltpu.VMEM((4, 2, VIS, KB), BF16),
            pltpu.VMEM((4, 2, VIS, KB), BF16),
            pltpu.VMEM((2, VIS, KB), BF16),
            pltpu.VMEM((4, 2, VIS, KB), BF16),
            pltpu.VMEM((2, HALF, KB), F32),
            pltpu.VMEM((2, HALF, KVW), F32),
            dma((4,)),
            dma((4, 8)), dma((4, 8)),
            dma((4,)), dma((4,)),
            dma((4, 3)), dma((4, 3)),
            dma((4, 4)), dma((4, 4)),
            dma((7,)), dma((7,)),
            dma((7,)), dma((7,)),
            dma((4,)), dma((4,)),
            dma((4,)), dma((4,)),
            dma((7,)), dma((7,)),
        ],
        compiler_params=pltpu.CompilerParams(
            collective_id=0, has_side_effects=True, vmem_limit_bytes=58 * 2**20
        ),
        cost_estimate=pl.CostEstimate(
            flops=14 * 10**9, bytes_accessed=30 * 10**6, transcendentals=0
        ),
        name="gather",
    )(img, cw, cb, lg, lb, cbias, gain, conn, w, kv, text)


def attend_kernel(group, length, q_ref, t_ref, v_ref, own_ref, out_ref, cache_ref, vis_ref):
    n = length[pl.program_id(0)]
    seg = q_ref.shape[1]
    live = lax.broadcasted_iota(jnp.int32, (seg, 1), 0) < n
    text = jnp.where(live, t_ref[0].astype(F32), 0.0).astype(BF16)
    cache_ref[0] = text.reshape(seg, 2, HD)

    @pl.when(pl.program_id(0) == 0)
    def _():
        vis_ref[...] = own_ref[...].reshape(VIS, 2, HD)

    vis = v_ref[0]
    half = (vis[:, HD:].astype(F32) * 0.5).astype(BF16)
    keys = jnp.concatenate([text[:, :HD], vis[:, :HD], vis[:, :HD]], axis=0)
    vals = jnp.concatenate([text[:, HD:], half, half], axis=0)
    row = lax.broadcasted_iota(jnp.int32, (2 * seg, HD), 0)
    ones = jnp.where(row < seg, 1.0, 0.5).astype(BF16)
    vals = jnp.concatenate([vals, ones], axis=1)
    nt = (((1,), (1,)), ((), ()))
    q = jnp.concatenate([q_ref[0, :, g * HD : (g + 1) * HD] for g in range(GQ)], axis=0)
    qi = lax.broadcasted_iota(jnp.int32, (seg, seg), 0)
    ki = lax.broadcasted_iota(jnp.int32, (seg, seg), 1)
    hidden = jnp.concatenate([jnp.where(ki <= qi, 0.0, -1e30)] * GQ, axis=0)
    s = lax.dot_general(q, keys, nt, preferred_element_type=F32)
    st = s[:, :seg] + hidden
    sv = s[:, seg:]
    peak = jnp.max(jnp.maximum(st, sv), axis=-1, keepdims=True)
    scale = HD ** (-0.5) * LOG2E
    e = jnp.concatenate([jnp.exp2((st - peak) * scale), jnp.exp2((sv - peak) * scale)], axis=1)
    o = jnp.dot(e.astype(BF16), vals, preferred_element_type=F32)
    o = o[:, :HD] / o[:, HD:]
    for g in range(GQ):
        out_ref[0, :, g * HD : (g + 1) * HD] = jnp.where(
            live, o[g * seg : (g + 1) * seg], 0.0
        ).astype(BF16)


def attend_call(group, length, q, tkv, vis, own):
    n, seg = q.shape[0], q.shape[1]
    return pl.pallas_call(
        attend_kernel,
        out_shape=(
            jax.ShapeDtypeStruct((n, seg, KB), BF16),
            jax.ShapeDtypeStruct((n, seg, 2, HD), BF16),
            jax.ShapeDtypeStruct((VIS, 2, HD), BF16),
        ),
        grid_spec=pltpu.PrefetchScalarGridSpec(
            num_scalar_prefetch=2,
            grid=(n,),
            in_specs=[
                pl.BlockSpec((1, seg, KB), lambda r, s, l: (r, 0, 0)),
                pl.BlockSpec((1, seg, KVW), lambda r, s, l: (r, 0, 0)),
                pl.BlockSpec((1, VIS, KVW), lambda r, s, l: (s[r] % 2 * 16 + s[r] // 2, 0, 0)),
                pl.BlockSpec((VIS, KVW), lambda r, s, l: (0, 0)),
            ],
            out_specs=(
                pl.BlockSpec((1, seg, KB), lambda r, s, l: (r, 0, 0)),
                pl.BlockSpec((1, seg, 2, HD), lambda r, s, l: (r, 0, 0, 0)),
                pl.BlockSpec((VIS, 2, HD), lambda r, s, l: (0, 0, 0)),
            ),
        ),
        name="attend",
    )(group, length, q, tkv, vis, own)


def per_device(
    image_map, conv_weight, conv_bias, ln_gain, ln_bias, connector, connector_bias,
    norm_gain, q_weight, kv_weight, text_hidden, rollout_group, text_length,
):
    rollouts, seg = text_hidden.shape[0], text_hidden.shape[1]
    q, tkv, own, vis = gather_call(
        image_map.reshape(SIDE, SIDE, CL), conv_weight,
        conv_bias, ln_gain, ln_bias,
        connector_bias.reshape(1, D), norm_gain.reshape(1, D), connector, q_weight,
        kv_weight.reshape(D, 2, HD), text_hidden.reshape(4, QUART, KB),
    )
    attended, cache, own = attend_call(
        rollout_group, text_length, q.reshape(rollouts, seg, KB), tkv.reshape(rollouts, seg, KVW),
        vis.reshape(32, VIS, KVW), own,
    )
    return (
        attended,
        cache.reshape(rollouts, seg, 1, 2, HD),
        own.reshape(1, VIS, 1, 2, HD),
    )


def solution(mesh):
    in_specs = (
        P("dp", None, None, "mp"),
        P(None, None, "mp"),
        P("mp"),
        P("mp"),
        P("mp"),
        P("mp", None),
        P(),
        P(),
        P("dp", "mp"),
        P(None, "mp", None, None),
        P("dp", None, "mp"),
        P("dp"),
        P("dp"),
    )
    out_specs = (
        P("dp", None, "mp"),
        P("dp", None, "mp", None, None),
        P("dp", None, "mp", None, None),
    )
    return jax.shard_map(
        per_device, mesh=mesh, in_specs=in_specs, out_specs=out_specs, check_vma=False
    )
```

```python
import functools

import jax
import jax.numpy as jnp
from jax import lax
from jax.experimental import pallas as pl
from jax.experimental.pallas import tpu as pltpu
from jax.sharding import PartitionSpec as P

MESH = pl.DeviceIdType.MESH
F32 = jnp.float32
BF16 = jnp.bfloat16

D = 7168
C = 3072
HD = 128
KSZ = 7
GQ = 7
SIDE = 16
VIS = 64
KB = 896
ROWS = 768
HALF = 384
QUART = 192
EIGHTH = 96
LOG2E = 1.4426950408889634
WR = 224
KVW = 256
CL = 384

A_L, A_R, A_Z, B_L, B_R, C_L, C_R, D_Z = range(8)


def gather_kernel(
    img, cw, cb, lg, lb, cbias, gain, conn_hbm, w_hbm, kv_hbm, x_hbm,
    q_out, tkv_out, own_out, vis_out,
    xraw, xbuf, wbuf, kvraw, kvbuf, connbuf, pad, conv, stats, ssb, part, rsb, pair, agb, qacc, kvacc,
    loc, x_s, x_r, w1_s, w1_r, w2_s, w2_r, wc_s, wc_r, st_s, st_r, ss_s, ss_r,
    rs_s, rs_r, ag_s, ag_r, v_s, v_r,
):
    dp = lax.axis_index("dp")
    mp = lax.axis_index("mp")
    y, zh, c = dp // 8, (dp // 2) % 4, dp % 2
    zl, x = mp // 4, mp % 4
    other = 1 - zl

    def mp_id(xx, zz):
        return zz * 4 + (xx + 4) % 4

    def dp_id(yy, zz, cc):
        return ((yy + 4) % 4) * 8 + ((zz + 4) % 4) * 2 + cc

    right, left, cross = (dp, mp_id(x + 1, zl)), (dp, mp_id(x - 1, zl)), (dp, mp_id(x, other))
    z_peer = [(dp_id(y, zh + d, c), mp) for d in (1, 2, 3)]
    y_peer = [(dp_id(y + d, zh, c), mp) for d in (1, 2, 3)]
    sib = (dp_id(y, zh, 1 - c), mp)
    mp_peer = [(dp, (mp + d) % 8) for d in range(1, 8)]

    def rcopy(src, dst, s, r, dev):
        return pltpu.make_async_remote_copy(src, dst, s, r, device_id=dev, device_id_type=MESH)

    bar = pltpu.get_barrier_semaphore()
    peers = mp_peer + z_peer + y_peer + [sib]
    for dev in peers:
        pl.semaphore_signal(bar, inc=1, device_id=dev, device_id_type=MESH)

    lc_x = pltpu.make_async_copy(x_hbm, xraw, loc.at[0])
    lc_w = pltpu.make_async_copy(w_hbm, wbuf.at[dp], loc.at[1])
    lc_kv = pltpu.make_async_copy(kv_hbm, kvraw, loc.at[2])
    lc_cn = pltpu.make_async_copy(conn_hbm, connbuf, loc.at[3])
    for cp in (lc_x, lc_w, lc_cn, lc_kv):
        cp.start()

    def gain_of(k):
        return gain[:, pl.ds(pl.multiple_of(k * KB, 128), KB)]

    lc_x.wait()
    for h in range(4):
        xbuf[mp, h] = (xraw[h].astype(F32) * gain_of(mp)).astype(BF16)

    pl.semaphore_wait(bar, len(peers))

    sends = []

    def go(cp):
        cp.start()
        sends.append(cp)

    def xcopy(h, slot, k, r0, rn, dev):
        piece = xbuf.at[k, h, pl.ds(r0, rn)]
        return rcopy(piece, piece, x_s.at[h, slot], x_r.at[h, slot], dev)

    def xsend(h, slot, k, r0, rn, dev):
        go(xcopy(h, slot, k, r0, rn, dev))

    def xrecv(h, slot, k, r0, rn):
        xcopy(h, slot, k, r0, rn, left).wait_recv()

    kl, kr, k2 = mp_id(x - 1, zl), mp_id(x + 1, zl), mp_id(x + 2, zl)
    kz, klz, krz, k2z = mp_id(x, other), mp_id(x - 1, other), mp_id(x + 1, other), mp_id(x + 2, other)

    x_peer = [(dp, mp_id(x + d, zl)) for d in (1, 2, 3)]

    def send_a(h):
        xsend(h, A_L, mp, 0, QUART, right)
        xsend(h, A_R, mp, 0, QUART, left)

    def send_az(h):
        xsend(h, A_Z, mp, 0, QUART, cross)

    def forward_b(h):
        xrecv(h, A_L, kl, 0, QUART)
        xsend(h, B_L, kl, 0, EIGHTH, right)
        xrecv(h, A_R, kr, 0, QUART)
        xsend(h, B_R, kr, EIGHTH, EIGHTH, left)

    def forward_c(h):
        xrecv(h, A_Z, kz, 0, QUART)
        xsend(h, C_L, kz, 0, QUART, right)
        xsend(h, C_R, kz, 0, QUART, left)

    def forward_d(h):
        xrecv(h, B_L, k2, 0, EIGHTH)
        xrecv(h, B_R, k2, EIGHTH, EIGHTH)
        xsend(h, D_Z, k2, 0, QUART, cross)

    def last_x(h):
        xrecv(h, C_L, klz, 0, QUART)
        xrecv(h, C_R, krz, 0, QUART)
        xrecv(h, D_Z, k2z, 0, QUART)

    def wslot(i):
        return wbuf.at[i]

    def wsend(src, i, s, r, dev):
        go(rcopy(src, wslot(i), s, r, dev))

    def wrecv(i, s, r):
        rcopy(wslot(i), wslot(i), s, r, sib).wait_recv()

    def half_w(i, p):
        return wbuf.at[i, pl.ds(p * (WR // 2), WR // 2)]

    zup, zdown = z_peer[0], z_peer[2]
    i_up, i_down, i_far = dp_id(y, zh + 1, c), dp_id(y, zh - 1, c), dp_id(y, zh + 2, c)
    wsend(w_hbm, dp, w1_s.at[0], w1_r.at[0], zup)
    wsend(w_hbm, dp, w1_s.at[1], w1_r.at[1], zdown)
    send_a(0)
    send_a(1)
    for d in range(3):
        wsend(w_hbm, dp, w2_s.at[0, d], w2_r.at[0, d], y_peer[d])
    wsend(w_hbm, dp, wc_s.at[0, 0], wc_r.at[0, 0], sib)

    pad[...] = jnp.zeros_like(pad)
    pad[3:19, 8:24, :] = img[...].astype(F32)

    def conv_lanes(l, carry):
        lanes = pl.ds(pl.multiple_of(l * 128, 128), 128)
        acc = jnp.zeros((SIDE, SIDE, 128), F32)
        taps = cw[:, :, lanes].astype(F32)
        for j in range(KSZ):
            cols = pad[:, 5 + j : 21 + j, lanes]
            for i in range(KSZ):
                acc = acc + cols[i : i + SIDE] * taps[i, j : j + 1].reshape(1, 1, 128)
        conv[:, lanes] = acc.reshape(SIDE * SIDE, 128)
        return carry

    lax.fori_loop(0, CL // 128, conv_lanes, 0)
    hi = lax.Precision.HIGHEST
    nt = (((1,), (1,)), ((), ()))
    ones = jnp.ones((8, CL), F32)
    cv = conv[...] + cb[...].reshape(1, CL)
    conv[...] = cv
    s1 = lax.dot_general(ones, cv, nt, precision=hi, preferred_element_type=F32)
    s2 = lax.dot_general(ones, cv * cv, nt, precision=hi, preferred_element_type=F32)
    stats[mp, 0:8] = s1
    stats[mp, 8:16] = s2
    for d in range(7):
        go(rcopy(stats.at[mp], stats.at[mp], st_s.at[d], st_r.at[d], mp_peer[d]))
    send_az(0)
    send_az(1)
    send_a(2)
    send_a(3)

    ones_b = jnp.ones((8, KB), BF16)
    for h in range(2):
        xv = xraw[2 * h : 2 * h + 2].reshape(HALF, KB).astype(F32)
        sq = xv * xv
        sq_hi = sq.astype(BF16)
        sq_lo = (sq - sq_hi.astype(F32)).astype(BF16)
        ssb[mp, :, h * HALF : (h + 1) * HALF] = lax.dot_general(
            ones_b, sq_hi, nt, preferred_element_type=F32
        ) + lax.dot_general(ones_b, sq_lo, nt, preferred_element_type=F32)
    for d in range(7):
        go(rcopy(ssb.at[mp], ssb.at[mp], ss_s.at[d], ss_r.at[d], mp_peer[d]))

    def src_of(d):
        return (mp + 7 - d) % 8

    def spread_w(e, i):
        for d in range(3):
            wsend(wslot(i), i, w2_s.at[e, d], w2_r.at[e, d], y_peer[d])
        wsend(wslot(i), i, wc_s.at[e, 0], wc_r.at[e, 0], sib)

    wrecv(i_down, w1_s.at[0], w1_r.at[0])
    go(rcopy(half_w(i_down, 0), half_w(i_down, 0), w1_s.at[2], w1_r.at[2], zup))
    spread_w(1, i_down)
    wrecv(i_up, w1_s.at[1], w1_r.at[1])
    go(rcopy(half_w(i_up, 1), half_w(i_up, 1), w1_s.at[3], w1_r.at[3], zdown))
    spread_w(2, i_up)
    send_az(2)

    for d in range(7):
        sd = src_of(d)
        rcopy(stats.at[sd], stats.at[sd], st_s.at[d], st_r.at[d], sib).wait_recv()
    tot = stats[0]
    for k in range(1, 8):
        tot = tot + stats[k]
    avg = tot[0:1] * (1.0 / C)
    var = tot[8:9] * (1.0 / C) - avg * avg
    rstd = lax.rsqrt(var + 1e-06)
    vrow = lax.broadcasted_iota(jnp.int32, (VIS, SIDE * SIDE), 0)
    pix = lax.broadcasted_iota(jnp.int32, (VIS, SIDE * SIDE), 1)
    hit = (vrow // 8 == pix // 32) & (vrow % 8 == (pix % 16) // 2)
    pool = jnp.where(hit, 0.25 * rstd, 0.0)
    shift = jnp.sum(pool * avg, axis=1, keepdims=True)
    mixed = jnp.dot(pool, conv[...], precision=hi, preferred_element_type=F32)
    pooled = ((mixed - shift) * lg[...].reshape(1, CL) + lb[...].reshape(1, CL)).astype(BF16)
    lc_cn.wait()

    def project(j):
        cols = pl.ds(pl.multiple_of(j * KB, 128), KB)
        return jnp.dot(pooled, connbuf[:, cols], preferred_element_type=F32)

    def pair_of(xx):
        own = project(mp_id(xx, zl))
        far = project(mp_id(xx, other))
        return own, far

    for d in range(3):
        own_p, far_p = pair_of(x + d + 1)
        xx = (x + d + 1) % 4
        part[xx, 0] = own_p.astype(BF16)
        part[xx, 1] = far_p.astype(BF16)
        go(rcopy(part.at[xx], rsb.at[x], rs_s.at[d], rs_r.at[d], x_peer[d]))
    near_sum, far_sum = pair_of(x)

    rcopy(half_w(i_far, 0), half_w(i_far, 0), w1_s.at[2], w1_r.at[2], sib).wait_recv()
    rcopy(half_w(i_far, 1), half_w(i_far, 1), w1_s.at[3], w1_r.at[3], sib).wait_recv()
    spread_w(3, i_far)
    forward_b(0)
    forward_b(1)
    forward_b(2)
    forward_b(3)

    lc_kv.wait()

    def kv_flat(n, carry):
        rows = pl.ds(n * 256, 256)
        kvbuf[rows] = kvraw[rows].reshape(256, KVW)
        return carry

    lax.fori_loop(0, D // 256, kv_flat, 0)
    kvacc[...] = jnp.zeros_like(kvacc)
    qacc[...] = jnp.zeros_like(qacc)

    def x_half(h, k):
        return xbuf[k, pl.ds(h * 2, 2)].reshape(HALF, KB)

    def kv_unit(h, k):
        kvacc[h] += jnp.dot(x_half(h, k), kvbuf[pl.ds(k * KB, KB)], preferred_element_type=F32)

    def q_unit(h, k):
        w = wbuf[pl.ds(k * 4, 4)].reshape(KB, KB)
        qacc[h] += jnp.dot(x_half(h, k), w, preferred_element_type=F32)

    def each(fn, ks):
        def step(n, carry):
            h, m = n // len(ks), n % len(ks)
            k = ks[0]
            for t in range(1, len(ks)):
                k = jnp.where(m == t, ks[t], k)
            fn(h, k)
            return carry

        lax.fori_loop(0, 2 * len(ks), step, 0)

    each(kv_unit, [mp, kl, kr])

    def from_x(d):
        return (x + 3 - d) % 4

    for d in range(3):
        sx = from_x(d)
        rcopy(rsb.at[sx], rsb.at[sx], rs_s.at[d], rs_r.at[d], sib).wait_recv()
        near_sum = near_sum + rsb[sx, 0].astype(F32)
        far_sum = far_sum + rsb[sx, 1].astype(F32)
    pair[0] = far_sum.astype(BF16)
    go(rcopy(pair.at[0], pair.at[1], rs_s.at[3], rs_r.at[3], cross))
    rcopy(pair.at[0], pair.at[1], rs_s.at[3], rs_r.at[3], cross).wait_recv()
    summed = near_sum + pair[1].astype(F32) + cbias[:, pl.ds(pl.multiple_of(mp * KB, 128), KB)]
    agb[x, zl] = summed.astype(BF16)
    go(rcopy(agb.at[x, zl], agb.at[x, zl], ag_s.at[3], ag_r.at[3], cross))
    send_az(3)
    forward_d(0)
    rcopy(agb.at[x, other], agb.at[x, other], ag_s.at[3], ag_r.at[3], cross).wait_recv()
    for d in range(3):
        go(rcopy(agb.at[x], agb.at[x], ag_s.at[d], ag_r.at[d], x_peer[d]))

    forward_c(0)
    forward_c(1)
    forward_c(2)
    forward_d(1)
    forward_c(3)
    each(kv_unit, [kz])

    i_of = [dp, i_down, i_up, i_far]

    def at_y(i, d):
        return (i + 32 - 8 * d) % 32

    def hand_w(e):
        for d in range(3):
            i = at_y(i_of[e], d + 1)
            wrecv(i, w2_s.at[e, d], w2_r.at[e, d])
            wsend(wslot(i), i, wc_s.at[e, d + 1], wc_r.at[e, d + 1], sib)

    for e in range(3):
        hand_w(e)

    for d in range(3):
        sx = from_x(d)
        rcopy(agb.at[sx], agb.at[sx], ag_s.at[d], ag_r.at[d], sib).wait_recv()

    def vis_step(k, carry):
        acc, sq = carry
        vf = agb[k % 4, k // 4].astype(F32)
        sq = sq + jnp.sum(vf * vf, axis=1, keepdims=True)
        vg = (vf * gain_of(k)).astype(BF16)
        acc = acc + jnp.dot(vg, kvbuf[pl.ds(k * KB, KB)], preferred_element_type=F32)
        return acc, sq

    vacc, vsq = lax.fori_loop(0, 8, vis_step, (jnp.zeros((VIS, KVW), F32), jnp.zeros((VIS, 1), F32)))
    vkv = (vacc * lax.rsqrt(vsq * (1.0 / D) + 1e-05)).astype(BF16)
    own_out[...] = vkv
    vis_out[c, y, zh] = vkv
    for d in range(3):
        piece = vis_out.at[c, y, zh]
        go(rcopy(piece, piece, v_s.at[d], v_r.at[d], z_peer[d]))

    forward_d(2)
    forward_d(3)
    hand_w(3)
    for e in range(4):
        for d in range(4):
            i = at_y((i_of[e] // 2) * 2 + 1 - c, d)
            wrecv(i, wc_s.at[e, d], wc_r.at[e, d])
    lc_w.wait()

    each(kv_unit, [k2])
    each(q_unit, [mp, kl, kr, k2, kz])

    for d in range(3):
        piece = vis_out.at[c, y, (zh + 3 - d) % 4]
        rcopy(piece, piece, v_s.at[d], v_r.at[d], sib).wait_recv()
    for d in range(3):
        piece = vis_out.at[c, y]
        go(rcopy(piece, piece, v_s.at[3 + d], v_r.at[3 + d], y_peer[d]))

    def quarter(n):
        h, rows = n // 2, pl.ds(n % 2 * QUART, QUART)
        last_x(n)

        def step(m, carry):
            k = jnp.where(m == 0, klz, jnp.where(m == 1, krz, k2z))
            xq = xbuf[k, n]
            w = wbuf[pl.ds(k * 4, 4)].reshape(KB, KB)
            kvacc[h, rows] += jnp.dot(xq, kvbuf[pl.ds(k * KB, KB)], preferred_element_type=F32)
            qacc[h, rows] += jnp.dot(xq, w, preferred_element_type=F32)
            return carry

        lax.fori_loop(0, 3, step, 0)

    quarter(0)
    quarter(1)

    for d in range(3):
        piece = vis_out.at[c, (y + 3 - d) % 4]
        rcopy(piece, piece, v_s.at[3 + d], v_r.at[3 + d], sib).wait_recv()
    go(rcopy(vis_out.at[c], vis_out.at[c], v_s.at[6], v_r.at[6], sib))

    for d in range(7):
        sd = src_of(d)
        rcopy(ssb.at[sd], ssb.at[sd], ss_s.at[d], ss_r.at[d], sib).wait_recv()
    ss = ssb[0]
    for k in range(1, 8):
        ss = ss + ssb[k]
    inv = lax.rsqrt(ss * (1.0 / D) + 1e-05)
    inv = jnp.transpose(jnp.broadcast_to(inv[0:1], (128, ROWS)))

    def finish(n):
        h, rows = n // 2, pl.ds(n % 2 * QUART, QUART)
        scale = inv[n * QUART : (n + 1) * QUART, 0:1]
        q_out[h, rows] = (qacc[h, rows] * scale).astype(BF16)
        tkv_out[h, rows] = (kvacc[h, rows] * scale).astype(BF16)

    finish(0)
    finish(1)
    for n in (2, 3):
        quarter(n)
        finish(n)

    rcopy(vis_out.at[1 - c], vis_out.at[1 - c], v_s.at[6], v_r.at[6], sib).wait_recv()
    for cp in sends:
        cp.wait_send()


def gather_call(img, cw, cb, lg, lb, cbias, gain, conn, w, kv, text):
    vm = pl.BlockSpec(memory_space=pltpu.VMEM)
    hb = pl.BlockSpec(memory_space=pl.ANY)
    dma = pltpu.SemaphoreType.DMA
    return pl.pallas_call(
        gather_kernel,
        out_shape=(
            jax.ShapeDtypeStruct((2, HALF, KB), BF16),
            jax.ShapeDtypeStruct((2, HALF, KVW), BF16),
            jax.ShapeDtypeStruct((VIS, KVW), BF16),
            jax.ShapeDtypeStruct((2, 4, 4, VIS, KVW), BF16),
        ),
        in_specs=[vm] * 7 + [hb] * 4,
        out_specs=(vm,) * 4,
        scratch_shapes=[
            pltpu.VMEM((4, QUART, KB), BF16),
            pltpu.VMEM((8, 4, QUART, KB), BF16),
            pltpu.VMEM((32, WR, KB), BF16),
            pltpu.VMEM((D, 2, HD), BF16),
            pltpu.VMEM((D, KVW), BF16),
            pltpu.VMEM((CL, D), BF16),
            pltpu.VMEM((22, 32, CL), F32),
            pltpu.VMEM((SIDE * SIDE, CL), F32),
            pltpu.VMEM((8, 16, SIDE * SIDE), F32),
            pltpu.VMEM((8, 8, ROWS), F32),
            pltpu.VMEM((4, 2, VIS, KB), BF16),
            pltpu.VMEM((4, 2, VIS, KB), BF16),
            pltpu.VMEM((2, VIS, KB), BF16),
            pltpu.VMEM((4, 2, VIS, KB), BF16),
            pltpu.VMEM((2, HALF, KB), F32),
            pltpu.VMEM((2, HALF, KVW), F32),
            dma((4,)),
            dma((4, 8)), dma((4, 8)),
            dma((4,)), dma((4,)),
            dma((4, 3)), dma((4, 3)),
            dma((4, 4)), dma((4, 4)),
            dma((7,)), dma((7,)),
            dma((7,)), dma((7,)),
            dma((4,)), dma((4,)),
            dma((4,)), dma((4,)),
            dma((7,)), dma((7,)),
        ],
        compiler_params=pltpu.CompilerParams(
            collective_id=0, has_side_effects=True, vmem_limit_bytes=58 * 2**20
        ),
        cost_estimate=pl.CostEstimate(
            flops=14 * 10**9, bytes_accessed=30 * 10**6, transcendentals=0
        ),
        name="gather",
    )(img, cw, cb, lg, lb, cbias, gain, conn, w, kv, text)


PER = 3


def attend_kernel(group, length, q_ref, t_ref, *refs):
    vis_refs, own_ref, (out_ref, cache_ref, vis_ref) = refs[:PER], refs[PER], refs[PER + 1 :]
    seg = q_ref.shape[1]

    @pl.when(pl.program_id(0) == 0)
    def _():
        vis_ref[...] = own_ref[...].reshape(VIS, 2, HD)

    nt = (((1,), (1,)), ((), ()))
    row = lax.broadcasted_iota(jnp.int32, (2 * seg, HD), 0)
    ones = jnp.where(row < seg, 1.0, 0.5).astype(BF16)
    qi = lax.broadcasted_iota(jnp.int32, (seg, seg), 0)
    ki = lax.broadcasted_iota(jnp.int32, (seg, seg), 1)
    hidden = jnp.concatenate([jnp.where(ki <= qi, 0.0, -1e30)] * GQ, axis=0)
    scale = HD ** (-0.5) * LOG2E
    for r in range(PER):
        n = length[pl.program_id(0) * PER + r]
        live = lax.broadcasted_iota(jnp.int32, (seg, 1), 0) < n
        text = jnp.where(live, t_ref[r].astype(F32), 0.0).astype(BF16)
        cache_ref[r] = text.reshape(seg, 2, HD)
        vis = vis_refs[r][0]
        half = (vis[:, HD:].astype(F32) * 0.5).astype(BF16)
        keys = jnp.concatenate([text[:, :HD], vis[:, :HD], vis[:, :HD]], axis=0)
        vals = jnp.concatenate([text[:, HD:], half, half], axis=0)
        vals = jnp.concatenate([vals, ones], axis=1)
        q = jnp.concatenate([q_ref[r, :, g * HD : (g + 1) * HD] for g in range(GQ)], axis=0)
        s = lax.dot_general(q, keys, nt, preferred_element_type=F32)
        st = s[:, :seg] + hidden
        sv = s[:, seg:]
        peak = jnp.max(jnp.maximum(st, sv), axis=-1, keepdims=True)
        e = jnp.concatenate([jnp.exp2((st - peak) * scale), jnp.exp2((sv - peak) * scale)], axis=1)
        o = jnp.dot(e.astype(BF16), vals, preferred_element_type=F32)
        o = o[:, :HD] / o[:, HD:]
        for g in range(GQ):
            out_ref[r, :, g * HD : (g + 1) * HD] = jnp.where(
                live, o[g * seg : (g + 1) * seg], 0.0
            ).astype(BF16)


def vis_block(r):
    def place(i, s, l):
        g = s[i * PER + r]
        return (g % 2 * 16 + g // 2, 0, 0)

    return pl.BlockSpec((1, VIS, KVW), place)


def attend_call(group, length, q, tkv, vis, own):
    n, seg = q.shape[0], q.shape[1]
    return pl.pallas_call(
        attend_kernel,
        out_shape=(
            jax.ShapeDtypeStruct((n, seg, KB), BF16),
            jax.ShapeDtypeStruct((n, seg, 2, HD), BF16),
            jax.ShapeDtypeStruct((VIS, 2, HD), BF16),
        ),
        grid_spec=pltpu.PrefetchScalarGridSpec(
            num_scalar_prefetch=2,
            grid=(n // PER,),
            in_specs=[
                pl.BlockSpec((PER, seg, KB), lambda r, s, l: (r, 0, 0)),
                pl.BlockSpec((PER, seg, KVW), lambda r, s, l: (r, 0, 0)),
            ]
            + [vis_block(r) for r in range(PER)]
            + [pl.BlockSpec((VIS, KVW), lambda r, s, l: (0, 0))],
            out_specs=(
                pl.BlockSpec((PER, seg, KB), lambda r, s, l: (r, 0, 0)),
                pl.BlockSpec((PER, seg, 2, HD), lambda r, s, l: (r, 0, 0, 0)),
                pl.BlockSpec((VIS, 2, HD), lambda r, s, l: (0, 0, 0)),
            ),
        ),
        compiler_params=pltpu.CompilerParams(vmem_limit_bytes=58 * 2**20),
        name="attend",
    )(group, length, q, tkv, *([vis] * PER), own)


def per_device(
    image_map, conv_weight, conv_bias, ln_gain, ln_bias, connector, connector_bias,
    norm_gain, q_weight, kv_weight, text_hidden, rollout_group, text_length,
):
    rollouts, seg = text_hidden.shape[0], text_hidden.shape[1]
    q, tkv, own, vis = gather_call(
        image_map.reshape(SIDE, SIDE, CL), conv_weight,
        conv_bias, ln_gain, ln_bias,
        connector_bias.reshape(1, D), norm_gain.reshape(1, D), connector, q_weight,
        kv_weight.reshape(D, 2, HD), text_hidden.reshape(4, QUART, KB),
    )
    attended, cache, own = attend_call(
        rollout_group, text_length, q.reshape(rollouts, seg, KB), tkv.reshape(rollouts, seg, KVW),
        vis.reshape(32, VIS, KVW), own,
    )
    return (
        attended,
        cache.reshape(rollouts, seg, 1, 2, HD),
        own.reshape(1, VIS, 1, 2, HD),
    )


def solution(mesh):
    in_specs = (
        P("dp", None, None, "mp"),
        P(None, None, "mp"),
        P("mp"),
        P("mp"),
        P("mp"),
        P("mp", None),
        P(),
        P(),
        P("dp", "mp"),
        P(None, "mp", None, None),
        P("dp", None, "mp"),
        P("dp"),
        P("dp"),
    )
    out_specs = (
        P("dp", None, "mp"),
        P("dp", None, "mp", None, None),
        P("dp", None, "mp", None, None),
    )
    return jax.shard_map(
        per_device, mesh=mesh, in_specs=in_specs, out_specs=out_specs, check_vma=False
    )
```

```python
import functools

import jax
import jax.numpy as jnp
from jax import lax
from jax.experimental import pallas as pl
from jax.experimental.pallas import tpu as pltpu
from jax.sharding import PartitionSpec as P

MESH = pl.DeviceIdType.MESH
F32 = jnp.float32
BF16 = jnp.bfloat16

D = 7168
C = 3072
HD = 128
KSZ = 7
GQ = 7
SIDE = 16
VIS = 64
KB = 896
ROWS = 768
HALF = 384
QUART = 192
EIGHTH = 96
LOG2E = 1.4426950408889634
WR = 224
KVW = 256
CL = 384

A_L, A_R, A_Z, B_L, B_R, C_L, C_R, D_Z = range(8)


def gather_kernel(
    img, cw, cb, lg, lb, cbias, gain, conn_hbm, w_hbm, kv_hbm, x_hbm,
    q_out, tkv_out, own_out, vis_out,
    xraw, xbuf, wbuf, kvraw, kvbuf, connbuf, pad, conv, stats, ssb, part, rsb, pair, agb, qacc, kvacc,
    loc, x_s, x_r, w1_s, w1_r, w2_s, w2_r, wc_s, wc_r, st_s, st_r, ss_s, ss_r,
    rs_s, rs_r, ag_s, ag_r, v_s, v_r,
):
    dp = lax.axis_index("dp")
    mp = lax.axis_index("mp")
    y, zh, c = dp // 8, (dp // 2) % 4, dp % 2
    zl, x = mp // 4, mp % 4
    other = 1 - zl

    def mp_id(xx, zz):
        return zz * 4 + (xx + 4) % 4

    def dp_id(yy, zz, cc):
        return ((yy + 4) % 4) * 8 + ((zz + 4) % 4) * 2 + cc

    right, left, cross = (dp, mp_id(x + 1, zl)), (dp, mp_id(x - 1, zl)), (dp, mp_id(x, other))
    z_peer = [(dp_id(y, zh + d, c), mp) for d in (1, 2, 3)]
    y_peer = [(dp_id(y + d, zh, c), mp) for d in (1, 2, 3)]
    sib = (dp_id(y, zh, 1 - c), mp)
    mp_peer = [(dp, (mp + d) % 8) for d in range(1, 8)]

    def rcopy(src, dst, s, r, dev):
        return pltpu.make_async_remote_copy(src, dst, s, r, device_id=dev, device_id_type=MESH)

    bar = pltpu.get_barrier_semaphore()
    peers = mp_peer + z_peer + y_peer + [sib]
    for dev in peers:
        pl.semaphore_signal(bar, inc=1, device_id=dev, device_id_type=MESH)

    lc_x = pltpu.make_async_copy(x_hbm, xraw, loc.at[0])
    lc_w = pltpu.make_async_copy(w_hbm, wbuf.at[dp], loc.at[1])
    lc_kv = pltpu.make_async_copy(kv_hbm, kvraw, loc.at[2])
    lc_cn = pltpu.make_async_copy(conn_hbm, connbuf, loc.at[3])
    for cp in (lc_x, lc_w, lc_cn, lc_kv):
        cp.start()

    def gain_of(k):
        return gain[:, pl.ds(pl.multiple_of(k * KB, 128), KB)]

    lc_x.wait()
    for h in range(4):
        xbuf[mp, h] = (xraw[h].astype(F32) * gain_of(mp)).astype(BF16)

    pad[...] = jnp.zeros_like(pad)
    pad[3:19, 8:24, :] = img[...].astype(F32)

    pl.semaphore_wait(bar, len(peers))

    sends = []

    def go(cp):
        cp.start()
        sends.append(cp)

    def xcopy(h, slot, k, r0, rn, dev):
        piece = xbuf.at[k, h, pl.ds(r0, rn)]
        return rcopy(piece, piece, x_s.at[h, slot], x_r.at[h, slot], dev)

    def xsend(h, slot, k, r0, rn, dev):
        go(xcopy(h, slot, k, r0, rn, dev))

    def xrecv(h, slot, k, r0, rn):
        xcopy(h, slot, k, r0, rn, left).wait_recv()

    kl, kr, k2 = mp_id(x - 1, zl), mp_id(x + 1, zl), mp_id(x + 2, zl)
    kz, klz, krz, k2z = mp_id(x, other), mp_id(x - 1, other), mp_id(x + 1, other), mp_id(x + 2, other)

    x_peer = [(dp, mp_id(x + d, zl)) for d in (1, 2, 3)]

    def send_a(h):
        xsend(h, A_L, mp, 0, QUART, right)
        xsend(h, A_R, mp, 0, QUART, left)

    def send_az(h):
        xsend(h, A_Z, mp, 0, QUART, cross)

    def forward_b(h):
        xrecv(h, A_L, kl, 0, QUART)
        xsend(h, B_L, kl, 0, EIGHTH, right)
        xrecv(h, A_R, kr, 0, QUART)
        xsend(h, B_R, kr, EIGHTH, EIGHTH, left)

    def forward_c(h):
        xrecv(h, A_Z, kz, 0, QUART)
        xsend(h, C_L, kz, 0, QUART, right)
        xsend(h, C_R, kz, 0, QUART, left)

    def forward_d(h):
        xrecv(h, B_L, k2, 0, EIGHTH)
        xrecv(h, B_R, k2, EIGHTH, EIGHTH)
        xsend(h, D_Z, k2, 0, QUART, cross)

    def last_x(h):
        xrecv(h, C_L, klz, 0, QUART)
        xrecv(h, C_R, krz, 0, QUART)
        xrecv(h, D_Z, k2z, 0, QUART)

    def wslot(i):
        return wbuf.at[i]

    def wsend(src, i, s, r, dev):
        go(rcopy(src, wslot(i), s, r, dev))

    def wrecv(i, s, r):
        rcopy(wslot(i), wslot(i), s, r, sib).wait_recv()

    def half_w(i, p):
        return wbuf.at[i, pl.ds(p * (WR // 2), WR // 2)]

    zup, zdown = z_peer[0], z_peer[2]
    i_up, i_down, i_far = dp_id(y, zh + 1, c), dp_id(y, zh - 1, c), dp_id(y, zh + 2, c)
    wsend(w_hbm, dp, w1_s.at[0], w1_r.at[0], zup)
    wsend(w_hbm, dp, w1_s.at[1], w1_r.at[1], zdown)
    send_a(0)
    send_a(1)
    for d in range(3):
        wsend(w_hbm, dp, w2_s.at[0, d], w2_r.at[0, d], y_peer[d])
    wsend(w_hbm, dp, wc_s.at[0, 0], wc_r.at[0, 0], sib)

    def conv_lanes(l, carry):
        lanes = pl.ds(pl.multiple_of(l * 128, 128), 128)
        acc = jnp.zeros((SIDE, SIDE, 128), F32)
        taps = cw[:, :, lanes].astype(F32)
        for j in range(KSZ):
            cols = pad[:, 5 + j : 21 + j, lanes]
            for i in range(KSZ):
                acc = acc + cols[i : i + SIDE] * taps[i, j : j + 1].reshape(1, 1, 128)
        conv[:, lanes] = acc.reshape(SIDE * SIDE, 128)
        return carry

    lax.fori_loop(0, CL // 128, conv_lanes, 0)
    hi = lax.Precision.HIGHEST
    nt = (((1,), (1,)), ((), ()))
    ones = jnp.ones((8, CL), F32)
    cv = conv[...] + cb[...].reshape(1, CL)
    conv[...] = cv
    s1 = lax.dot_general(ones, cv, nt, precision=hi, preferred_element_type=F32)
    s2 = lax.dot_general(ones, cv * cv, nt, precision=hi, preferred_element_type=F32)
    stats[mp, 0:8] = s1
    stats[mp, 8:16] = s2
    for d in range(7):
        go(rcopy(stats.at[mp], stats.at[mp], st_s.at[d], st_r.at[d], mp_peer[d]))
    send_az(0)
    send_az(1)
    send_a(2)
    send_a(3)

    ones_b = jnp.ones((8, KB), BF16)
    for h in range(2):
        xv = xraw[2 * h : 2 * h + 2].reshape(HALF, KB).astype(F32)
        sq = xv * xv
        sq_hi = sq.astype(BF16)
        sq_lo = (sq - sq_hi.astype(F32)).astype(BF16)
        ssb[mp, :, h * HALF : (h + 1) * HALF] = lax.dot_general(
            ones_b, sq_hi, nt, preferred_element_type=F32
        ) + lax.dot_general(ones_b, sq_lo, nt, preferred_element_type=F32)
    for d in range(7):
        go(rcopy(ssb.at[mp], ssb.at[mp], ss_s.at[d], ss_r.at[d], mp_peer[d]))

    def src_of(d):
        return (mp + 7 - d) % 8

    def spread_w(e, i):
        for d in range(3):
            wsend(wslot(i), i, w2_s.at[e, d], w2_r.at[e, d], y_peer[d])
        wsend(wslot(i), i, wc_s.at[e, 0], wc_r.at[e, 0], sib)

    wrecv(i_down, w1_s.at[0], w1_r.at[0])
    go(rcopy(half_w(i_down, 0), half_w(i_down, 0), w1_s.at[2], w1_r.at[2], zup))
    spread_w(1, i_down)
    wrecv(i_up, w1_s.at[1], w1_r.at[1])
    go(rcopy(half_w(i_up, 1), half_w(i_up, 1), w1_s.at[3], w1_r.at[3], zdown))
    spread_w(2, i_up)
    send_az(2)

    for d in range(7):
        sd = src_of(d)
        rcopy(stats.at[sd], stats.at[sd], st_s.at[d], st_r.at[d], sib).wait_recv()
    tot = stats[0]
    for k in range(1, 8):
        tot = tot + stats[k]
    avg = tot[0:1] * (1.0 / C)
    var = tot[8:9] * (1.0 / C) - avg * avg
    rstd = lax.rsqrt(var + 1e-06)
    vrow = lax.broadcasted_iota(jnp.int32, (VIS, SIDE * SIDE), 0)
    pix = lax.broadcasted_iota(jnp.int32, (VIS, SIDE * SIDE), 1)
    hit = (vrow // 8 == pix // 32) & (vrow % 8 == (pix % 16) // 2)
    pool = jnp.where(hit, 0.25 * rstd, 0.0)
    shift = jnp.sum(pool * avg, axis=1, keepdims=True)
    mixed = jnp.dot(pool, conv[...], precision=hi, preferred_element_type=F32)
    pooled = ((mixed - shift) * lg[...].reshape(1, CL) + lb[...].reshape(1, CL)).astype(BF16)
    lc_cn.wait()

    def project(j):
        cols = pl.ds(pl.multiple_of(j * KB, 128), KB)
        return jnp.dot(pooled, connbuf[:, cols], preferred_element_type=F32)

    def pair_of(xx):
        own = project(mp_id(xx, zl))
        far = project(mp_id(xx, other))
        return own, far

    for d in range(3):
        own_p, far_p = pair_of(x + d + 1)
        xx = (x + d + 1) % 4
        part[xx, 0] = own_p.astype(BF16)
        part[xx, 1] = far_p.astype(BF16)
        go(rcopy(part.at[xx], rsb.at[x], rs_s.at[d], rs_r.at[d], x_peer[d]))
    near_sum, far_sum = pair_of(x)

    rcopy(half_w(i_far, 0), half_w(i_far, 0), w1_s.at[2], w1_r.at[2], sib).wait_recv()
    rcopy(half_w(i_far, 1), half_w(i_far, 1), w1_s.at[3], w1_r.at[3], sib).wait_recv()
    spread_w(3, i_far)
    forward_b(0)
    forward_b(1)
    forward_b(2)
    forward_b(3)

    lc_kv.wait()

    def kv_flat(n, carry):
        rows = pl.ds(n * 256, 256)
        kvbuf[rows] = kvraw[rows].reshape(256, KVW)
        return carry

    lax.fori_loop(0, D // 256, kv_flat, 0)
    kvacc[...] = jnp.zeros_like(kvacc)
    qacc[...] = jnp.zeros_like(qacc)

    def x_half(h, k):
        return xbuf[k, pl.ds(h * 2, 2)].reshape(HALF, KB)

    def kv_unit(h, k):
        kvacc[h] += jnp.dot(x_half(h, k), kvbuf[pl.ds(k * KB, KB)], preferred_element_type=F32)

    def q_unit(h, k):
        w = wbuf[pl.ds(k * 4, 4)].reshape(KB, KB)
        qacc[h] += jnp.dot(x_half(h, k), w, preferred_element_type=F32)

    def each(fn, ks):
        def step(n, carry):
            h, m = n // len(ks), n % len(ks)
            k = ks[0]
            for t in range(1, len(ks)):
                k = jnp.where(m == t, ks[t], k)
            fn(h, k)
            return carry

        lax.fori_loop(0, 2 * len(ks), step, 0)

    each(kv_unit, [mp, kl, kr])

    def from_x(d):
        return (x + 3 - d) % 4

    for d in range(3):
        sx = from_x(d)
        rcopy(rsb.at[sx], rsb.at[sx], rs_s.at[d], rs_r.at[d], sib).wait_recv()
        near_sum = near_sum + rsb[sx, 0].astype(F32)
        far_sum = far_sum + rsb[sx, 1].astype(F32)
    pair[0] = far_sum.astype(BF16)
    go(rcopy(pair.at[0], pair.at[1], rs_s.at[3], rs_r.at[3], cross))
    rcopy(pair.at[0], pair.at[1], rs_s.at[3], rs_r.at[3], cross).wait_recv()
    summed = near_sum + pair[1].astype(F32) + cbias[:, pl.ds(pl.multiple_of(mp * KB, 128), KB)]
    agb[x, zl] = summed.astype(BF16)
    go(rcopy(agb.at[x, zl], agb.at[x, zl], ag_s.at[3], ag_r.at[3], cross))
    send_az(3)
    forward_d(0)
    rcopy(agb.at[x, other], agb.at[x, other], ag_s.at[3], ag_r.at[3], cross).wait_recv()
    for d in range(3):
        go(rcopy(agb.at[x], agb.at[x], ag_s.at[d], ag_r.at[d], x_peer[d]))

    forward_c(0)
    forward_c(1)
    forward_c(2)
    forward_d(1)
    forward_c(3)
    each(kv_unit, [kz])

    i_of = [dp, i_down, i_up, i_far]

    def at_y(i, d):
        return (i + 32 - 8 * d) % 32

    def hand_w(e):
        for d in range(3):
            i = at_y(i_of[e], d + 1)
            wrecv(i, w2_s.at[e, d], w2_r.at[e, d])
            wsend(wslot(i), i, wc_s.at[e, d + 1], wc_r.at[e, d + 1], sib)

    for e in range(3):
        hand_w(e)

    for d in range(3):
        sx = from_x(d)
        rcopy(agb.at[sx], agb.at[sx], ag_s.at[d], ag_r.at[d], sib).wait_recv()

    def vis_step(k, carry):
        acc, sq = carry
        vf = agb[k % 4, k // 4].astype(F32)
        sq = sq + jnp.sum(vf * vf, axis=1, keepdims=True)
        vg = (vf * gain_of(k)).astype(BF16)
        acc = acc + jnp.dot(vg, kvbuf[pl.ds(k * KB, KB)], preferred_element_type=F32)
        return acc, sq

    vacc, vsq = lax.fori_loop(0, 8, vis_step, (jnp.zeros((VIS, KVW), F32), jnp.zeros((VIS, 1), F32)))
    vkv = (vacc * lax.rsqrt(vsq * (1.0 / D) + 1e-05)).astype(BF16)
    own_out[...] = vkv
    vis_out[c, y, zh] = vkv
    for d in range(3):
        piece = vis_out.at[c, y, zh]
        go(rcopy(piece, piece, v_s.at[d], v_r.at[d], z_peer[d]))

    forward_d(2)
    forward_d(3)
    hand_w(3)
    for d in range(3):
        piece = vis_out.at[c, y, (zh + 3 - d) % 4]
        rcopy(piece, piece, v_s.at[d], v_r.at[d], sib).wait_recv()
    for d in range(3):
        piece = vis_out.at[c, y]
        go(rcopy(piece, piece, v_s.at[3 + d], v_r.at[3 + d], y_peer[d]))

    for e in range(4):
        for d in range(4):
            i = at_y((i_of[e] // 2) * 2 + 1 - c, d)
            wrecv(i, wc_s.at[e, d], wc_r.at[e, d])
    lc_w.wait()

    each(kv_unit, [k2])
    each(q_unit, [mp, kl, kr, k2, kz])

    for d in range(3):
        piece = vis_out.at[c, (y + 3 - d) % 4]
        rcopy(piece, piece, v_s.at[3 + d], v_r.at[3 + d], sib).wait_recv()
    go(rcopy(vis_out.at[c], vis_out.at[c], v_s.at[6], v_r.at[6], sib))


    def quarter(n):
        h, rows = n // 2, pl.ds(n % 2 * QUART, QUART)
        last_x(n)

        def step(m, carry):
            k = jnp.where(m == 0, klz, jnp.where(m == 1, krz, k2z))
            xq = xbuf[k, n]
            w = wbuf[pl.ds(k * 4, 4)].reshape(KB, KB)
            kvacc[h, rows] += jnp.dot(xq, kvbuf[pl.ds(k * KB, KB)], preferred_element_type=F32)
            qacc[h, rows] += jnp.dot(xq, w, preferred_element_type=F32)
            return carry

        lax.fori_loop(0, 3, step, 0)

    quarter(0)
    quarter(1)

    for d in range(7):
        sd = src_of(d)
        rcopy(ssb.at[sd], ssb.at[sd], ss_s.at[d], ss_r.at[d], sib).wait_recv()
    ss = ssb[0]
    for k in range(1, 8):
        ss = ss + ssb[k]
    inv = lax.rsqrt(ss * (1.0 / D) + 1e-05)
    inv = jnp.transpose(jnp.broadcast_to(inv[0:1], (128, ROWS)))

    def finish(n):
        h, rows = n // 2, pl.ds(n % 2 * QUART, QUART)
        scale = inv[n * QUART : (n + 1) * QUART, 0:1]
        q_out[h, rows] = (qacc[h, rows] * scale).astype(BF16)
        tkv_out[h, rows] = (kvacc[h, rows] * scale).astype(BF16)

    finish(0)
    finish(1)
    for n in (2, 3):
        quarter(n)
        finish(n)

    rcopy(vis_out.at[1 - c], vis_out.at[1 - c], v_s.at[6], v_r.at[6], sib).wait_recv()
    for cp in sends:
        cp.wait_send()


def gather_call(img, cw, cb, lg, lb, cbias, gain, conn, w, kv, text):
    vm = pl.BlockSpec(memory_space=pltpu.VMEM)
    hb = pl.BlockSpec(memory_space=pl.ANY)
    dma = pltpu.SemaphoreType.DMA
    return pl.pallas_call(
        gather_kernel,
        out_shape=(
            jax.ShapeDtypeStruct((2, HALF, KB), BF16),
            jax.ShapeDtypeStruct((2, HALF, KVW), BF16),
            jax.ShapeDtypeStruct((VIS, KVW), BF16),
            jax.ShapeDtypeStruct((2, 4, 4, VIS, KVW), BF16),
        ),
        in_specs=[vm] * 7 + [hb] * 4,
        out_specs=(vm,) * 4,
        scratch_shapes=[
            pltpu.VMEM((4, QUART, KB), BF16),
            pltpu.VMEM((8, 4, QUART, KB), BF16),
            pltpu.VMEM((32, WR, KB), BF16),
            pltpu.VMEM((D, 2, HD), BF16),
            pltpu.VMEM((D, KVW), BF16),
            pltpu.VMEM((CL, D), BF16),
            pltpu.VMEM((22, 32, CL), F32),
            pltpu.VMEM((SIDE * SIDE, CL), F32),
            pltpu.VMEM((8, 16, SIDE * SIDE), F32),
            pltpu.VMEM((8, 8, ROWS), F32),
            pltpu.VMEM((4, 2, VIS, KB), BF16),
            pltpu.VMEM((4, 2, VIS, KB), BF16),
            pltpu.VMEM((2, VIS, KB), BF16),
            pltpu.VMEM((4, 2, VIS, KB), BF16),
            pltpu.VMEM((2, HALF, KB), F32),
            pltpu.VMEM((2, HALF, KVW), F32),
            dma((4,)),
            dma((4, 8)), dma((4, 8)),
            dma((4,)), dma((4,)),
            dma((4, 3)), dma((4, 3)),
            dma((4, 4)), dma((4, 4)),
            dma((7,)), dma((7,)),
            dma((7,)), dma((7,)),
            dma((4,)), dma((4,)),
            dma((4,)), dma((4,)),
            dma((7,)), dma((7,)),
        ],
        compiler_params=pltpu.CompilerParams(
            collective_id=0, has_side_effects=True, vmem_limit_bytes=58 * 2**20
        ),
        cost_estimate=pl.CostEstimate(
            flops=14 * 10**9, bytes_accessed=30 * 10**6, transcendentals=0
        ),
        name="gather",
    )(img, cw, cb, lg, lb, cbias, gain, conn, w, kv, text)


PER = 3


def attend_kernel(group, length, q_ref, t_ref, *refs):
    vis_refs, own_ref, (out_ref, cache_ref, vis_ref) = refs[:PER], refs[PER], refs[PER + 1 :]
    seg = q_ref.shape[1]

    @pl.when(pl.program_id(0) == 0)
    def _():
        vis_ref[...] = own_ref[...].reshape(VIS, 2, HD)

    nt = (((1,), (1,)), ((), ()))
    row = lax.broadcasted_iota(jnp.int32, (2 * seg, HD), 0)
    ones = jnp.where(row < seg, 1.0, 0.5).astype(BF16)
    qi = lax.broadcasted_iota(jnp.int32, (seg, seg), 0)
    ki = lax.broadcasted_iota(jnp.int32, (seg, seg), 1)
    hidden = jnp.concatenate([jnp.where(ki <= qi, 0.0, -1e30)] * GQ, axis=0)
    scale = HD ** (-0.5) * LOG2E
    for r in range(PER):
        n = length[pl.program_id(0) * PER + r]
        live = lax.broadcasted_iota(jnp.int32, (seg, 1), 0) < n
        text = jnp.where(live, t_ref[r].astype(F32), 0.0).astype(BF16)
        cache_ref[r] = text.reshape(seg, 2, HD)
        vis = vis_refs[r][0]
        half = (vis[:, HD:].astype(F32) * 0.5).astype(BF16)
        keys = jnp.concatenate([text[:, :HD], vis[:, :HD], vis[:, :HD]], axis=0)
        vals = jnp.concatenate([text[:, HD:], half, half], axis=0)
        vals = jnp.concatenate([vals, ones], axis=1)
        q = jnp.concatenate([q_ref[r, :, g * HD : (g + 1) * HD] for g in range(GQ)], axis=0)
        s = lax.dot_general(q, keys, nt, preferred_element_type=F32)
        st = s[:, :seg] + hidden
        sv = s[:, seg:]
        peak = jnp.max(jnp.maximum(st, sv), axis=-1, keepdims=True)
        e = jnp.concatenate([jnp.exp2((st - peak) * scale), jnp.exp2((sv - peak) * scale)], axis=1)
        o = jnp.dot(e.astype(BF16), vals, preferred_element_type=F32)
        o = o[:, :HD] / o[:, HD:]
        for g in range(GQ):
            out_ref[r, :, g * HD : (g + 1) * HD] = jnp.where(
                live, o[g * seg : (g + 1) * seg], 0.0
            ).astype(BF16)


def vis_block(r):
    def place(i, s, l):
        g = s[i * PER + r]
        return (g % 2 * 16 + g // 2, 0, 0)

    return pl.BlockSpec((1, VIS, KVW), place)


def attend_call(group, length, q, tkv, vis, own):
    n, seg = q.shape[0], q.shape[1]
    return pl.pallas_call(
        attend_kernel,
        out_shape=(
            jax.ShapeDtypeStruct((n, seg, KB), BF16),
            jax.ShapeDtypeStruct((n, seg, 2, HD), BF16),
            jax.ShapeDtypeStruct((VIS, 2, HD), BF16),
        ),
        grid_spec=pltpu.PrefetchScalarGridSpec(
            num_scalar_prefetch=2,
            grid=(n // PER,),
            in_specs=[
                pl.BlockSpec((PER, seg, KB), lambda r, s, l: (r, 0, 0)),
                pl.BlockSpec((PER, seg, KVW), lambda r, s, l: (r, 0, 0)),
            ]
            + [vis_block(r) for r in range(PER)]
            + [pl.BlockSpec((VIS, KVW), lambda r, s, l: (0, 0))],
            out_specs=(
                pl.BlockSpec((PER, seg, KB), lambda r, s, l: (r, 0, 0)),
                pl.BlockSpec((PER, seg, 2, HD), lambda r, s, l: (r, 0, 0, 0)),
                pl.BlockSpec((VIS, 2, HD), lambda r, s, l: (0, 0, 0)),
            ),
        ),
        compiler_params=pltpu.CompilerParams(vmem_limit_bytes=58 * 2**20),
        name="attend",
    )(group, length, q, tkv, *([vis] * PER), own)


def per_device(
    image_map, conv_weight, conv_bias, ln_gain, ln_bias, connector, connector_bias,
    norm_gain, q_weight, kv_weight, text_hidden, rollout_group, text_length,
):
    rollouts, seg = text_hidden.shape[0], text_hidden.shape[1]
    q, tkv, own, vis = gather_call(
        image_map.reshape(SIDE, SIDE, CL), conv_weight,
        conv_bias, ln_gain, ln_bias,
        connector_bias.reshape(1, D), norm_gain.reshape(1, D), connector, q_weight,
        kv_weight.reshape(D, 2, HD), text_hidden.reshape(4, QUART, KB),
    )
    attended, cache, own = attend_call(
        rollout_group, text_length, q.reshape(rollouts, seg, KB), tkv.reshape(rollouts, seg, KVW),
        vis.reshape(32, VIS, KVW), own,
    )
    return (
        attended,
        cache.reshape(rollouts, seg, 1, 2, HD),
        own.reshape(1, VIS, 1, 2, HD),
    )


def solution(mesh):
    in_specs = (
        P("dp", None, None, "mp"),
        P(None, None, "mp"),
        P("mp"),
        P("mp"),
        P("mp"),
        P("mp", None),
        P(),
        P(),
        P("dp", "mp"),
        P(None, "mp", None, None),
        P("dp", None, "mp"),
        P("dp"),
        P("dp"),
    )
    out_specs = (
        P("dp", None, "mp"),
        P("dp", None, "mp", None, None),
        P("dp", None, "mp", None, None),
    )
    return jax.shard_map(
        per_device, mesh=mesh, in_specs=in_specs, out_specs=out_specs, check_vma=False
    )
```
